128 devices in a mesh: mp: 4 (over z_hi, core), dp: 32 (over y, x, z_lo).
Axes of the slice: x: 4, y: 4, z: 4 (z_hi: 2, z_lo: 2; z = z_hi * 2 + z_lo), core: 2. Of those that a mesh axis runs over, the one named last changes fastest.
Arguments:
- tokens: bfloat16 [512, 64, 1024], P('dp'), may hold values from -10 to 10
- norm_gain: float32 [1024], replicated, may hold values from 0.1 to 1.9
- weight_in: bfloat16 [1024, 4096], P(None, 'mp'), may hold values from -0.1875 to 0.1875
- weight_out: bfloat16 [4096, 1024], P('mp'), may hold values from -0.09375 to 0.09375
- final_gain: float32 [1024], replicated, may hold values from 0.1 to 1.9
- centres: bfloat16 [1048576, 1024], P(('mp', 'dp')), may hold values from -7 to 7
- labels: int32 [512], P('dp'), may hold values from 0 to 1048575
Outputs:
- row_loss: float32 [512], P('dp')
- feat_grad: float32 [512, 1024], P('dp', 'mp')
The draws below stay inside these ranges and needn't reach their ends.
All inputs are finite; a program needn't handle non-finite values.
Results may differ from the reference program's by a relative error of at most 0.0038.
Values may be sent and summed in bfloat16 or wider, within the bound.
No kernel may reach another device: no remote copies, remote signals or barrier semaphores. Data moves between devices by JAX's collectives and lax.ppermute only.
A program may use at most 128 MiB of HBM per device.

```python
import math
import jax
import jax.numpy as jnp
from jax import lax

D = 1024
FF = 4096
CLS_DEV = 8192
TOK = 64
IMAGES = 512
CLASSES = 1048576


def group_table(key):
    group_count = max(CLASSES // 256, 1)
    return jax.random.truncated_normal(jax.random.fold_in(key, 101), -4.0, 4.0, (group_count, D), jnp.float32)


def draw_tokens(key, part):
    table = group_table(key)
    group_count = table.shape[0]
    image_group = jax.random.randint(jax.random.fold_in(key, 103), (IMAGES,), 0, group_count).astype(jnp.int32)
    noise = jax.random.truncated_normal(jax.random.fold_in(key, 104), -4.0, 4.0, (IMAGES, TOK, D), jnp.float32)
    strength = jax.random.uniform(jax.random.fold_in(key, 105), (IMAGES,), jnp.float32, 0.0, 0.3)
    direction = table[image_group] * strength[:, None]
    return (noise + direction[:, None, :]).astype(jnp.bfloat16)


def draw_centres(key, part):
    table = group_table(key)
    group_count = table.shape[0]
    member_order = jax.random.permutation(jax.random.fold_in(key, 106), CLASSES).astype(jnp.int32)
    class_group = (member_order % group_count).astype(jnp.int32)
    block_count = CLASSES // CLS_DEV
    group_blocks = class_group.reshape(block_count, CLS_DEV)
    block_index = jnp.arange(block_count).astype(jnp.int32)
    block_key = jax.random.fold_in(key, 107)
    common = 0.26 * jax.random.truncated_normal(jax.random.fold_in(key, 108), -2.5, 2.5, (D,), jnp.float32)

    def one_block(inputs):
        block_groups, index = inputs
        sub_key = jax.random.fold_in(block_key, index)
        noise = jax.random.truncated_normal(jax.random.fold_in(sub_key, 1), -4.0, 4.0, (CLS_DEV, D), jnp.float32)
        pull = jax.random.uniform(jax.random.fold_in(sub_key, 2), (CLS_DEV,), jnp.float32, 0.0, 0.1)
        return noise + pull[:, None] * table[block_groups] + common[None, :]
    return lax.map(one_block, (group_blocks, block_index)).reshape(CLASSES, D).astype(jnp.bfloat16)


def plant(array, own_key, smallest, high):
    shape = array.shape
    index_at = [jax.random.randint(jax.random.fold_in(own_key, axis), (), 0, shape[axis]) for axis in range(len(shape))]
    array = array.at[tuple(index_at)].set(smallest)
    longest = shape.index(max(shape))
    index_at[longest] = (index_at[longest] + 1) % shape[longest]
    return array.at[tuple(index_at)].set(high)


def levels(stream_key, shape, cuts, least, top_value):
    factor_of, own = 1.0, jax.random.fold_in(stream_key, 6)
    for position, parts in cuts:
        heights = jnp.exp(jax.random.uniform(jax.random.fold_in(own, position), (parts,), jnp.float32, least / len(cuts), top_value / len(cuts)))
        factor_of = factor_of * jnp.repeat(heights, shape[position] // parts).reshape([-1 if axis == position else 1 for axis in range(len(shape))])
    return factor_of


def scatter_about(stream_key, shape, deviation, bound, pieces=(), held_as=jnp.bfloat16):
    array = jax.random.normal(stream_key, shape, jnp.float32) * deviation
    if len(pieces) > 0:
        array = levels(stream_key, shape, pieces, -0.22, 0.18) * array
    return jnp.clip(array, min=-bound, max=bound).astype(held_as)


def setup_inputs(seed: int = 0) -> dict:
    streams_of = jax.random.split(jax.random.key(seed), 8)
    return {
        "tokens": draw_tokens(jax.random.fold_in(streams_of[7], 71), 0),
        "norm_gain": jnp.clip(1.0 + 0.18 * jax.random.normal(streams_of[1], (D,), jnp.float32), 0.1, 1.9),
        "weight_in": scatter_about(streams_of[2], (D, FF), D ** -0.5, 0.1875, ((1, 4),)),
        "weight_out": scatter_about(streams_of[3], (FF, D), FF ** -0.5, 0.09375, ((0, 4),)),
        "final_gain": jnp.clip(1.0 + 0.18 * jax.random.normal(streams_of[4], (D,), jnp.float32), 0.1, 1.9),
        "centres": draw_centres(jax.random.fold_in(streams_of[7], 71), 0),
        "labels": plant(jax.random.randint(streams_of[6], (IMAGES,), 0, CLASSES), jax.random.fold_in(streams_of[6], 1), 0, CLASSES - 1).astype(jnp.int32),
    }


logit_scale = 64.0
angle_margin = 0.5

def layer_norm(values, gain_vec):
    average = lax.optimization_barrier(jnp.mean(values, axis=-1, keepdims=True))
    centred = values - average
    variance = lax.optimization_barrier(jnp.mean(centred * centred, axis=-1, keepdims=True))
    return centred * lax.rsqrt(variance + 1e-06) * gain_vec

def arc_target(target_cos):
    target_sine = jnp.sqrt(jnp.maximum(1.0 - target_cos * target_cos, 0.01))
    inside = target_cos > -math.cos(angle_margin)
    shifted = jnp.where(inside, target_cos * math.cos(angle_margin) - target_sine * math.sin(angle_margin), target_cos - angle_margin * math.sin(angle_margin))
    margin_slope = jnp.where(inside, math.cos(angle_margin) + math.sin(angle_margin) * target_cos / target_sine, 1.0)
    return (shifted, margin_slope)

def unit_centres(centre_block):
    block_wide = centre_block.astype(jnp.float32)
    return (block_wide * lax.rsqrt(lax.optimization_barrier(jnp.sum(block_wide * block_wide, axis=1, keepdims=True)) + 1e-06)).astype(jnp.bfloat16)

def block_logits(unit_rows, centre_unit, labels, offset):
    cosine = lax.dot_general(unit_rows, centre_unit, (((1,), (1,)), ((), ())), preferred_element_type=jnp.float32)
    local_label = labels - offset
    picked = local_label[:, None] == lax.broadcasted_iota(jnp.int32, cosine.shape, 1)
    target_cos = lax.optimization_barrier(jnp.sum(jnp.where(picked, cosine, 0.0), axis=1))
    shifted, margin_slope = arc_target(target_cos)
    logits = jnp.where(picked, logit_scale * shifted[:, None], logit_scale * cosine)
    is_owner = jnp.any(picked, axis=1)
    return (logits, picked, is_owner, shifted, margin_slope)

def reference(tokens, norm_gain, weight_in, weight_out, final_gain, centres, labels):
    model_width = tokens.shape[2]
    tokens_wide = tokens.astype(jnp.float32)
    normed = layer_norm(tokens_wide, norm_gain).astype(jnp.bfloat16).reshape(-1, model_width)
    hidden = jax.nn.gelu(jnp.dot(normed, weight_in, preferred_element_type=jnp.float32), approximate=False).astype(jnp.bfloat16)
    branch = jnp.dot(hidden, weight_out, preferred_element_type=jnp.float32).reshape(tokens.shape)
    pooled = lax.optimization_barrier(jnp.mean(tokens_wide, axis=1)) + lax.optimization_barrier(jnp.mean(branch, axis=1))
    embedding = layer_norm(pooled, final_gain)
    length = jnp.sqrt(lax.optimization_barrier(jnp.sum(embedding * embedding, axis=1)) + 1e-06)
    unit_rows = (embedding / length[:, None]).astype(jnp.bfloat16)
    blocks = centres.reshape(-1, CLS_DEV, model_width)
    block_ids = jnp.arange(blocks.shape[0]).astype(jnp.int32)

    def first_pass(carried, inputs):
        centre_block, block_index = inputs
        offset = (block_index * CLS_DEV).astype(jnp.int32)
        logits, picked, is_owner, shifted, margin_slope = block_logits(unit_rows, unit_centres(centre_block), labels, offset)
        totals = carried[0] + lax.optimization_barrier(jnp.sum(jnp.exp(logits), axis=1))
        target = carried[1] + jnp.where(is_owner, logit_scale * shifted, 0.0)
        return ((totals, target), None)
    zeros_rows = jnp.zeros((unit_rows.shape[0],), jnp.float32)
    (totals, target), _ = lax.scan(first_pass, (zeros_rows, zeros_rows), (blocks, block_ids))
    row_loss = jnp.log(totals) - target

    def second_pass(carried, inputs):
        centre_block, block_index = inputs
        offset = (block_index * CLS_DEV).astype(jnp.int32)
        centre_unit = unit_centres(centre_block)
        logits, picked, is_owner, shifted, margin_slope = block_logits(unit_rows, centre_unit, labels, offset)
        probability = jnp.exp(logits) / totals[:, None]
        weights = (logit_scale * jnp.where(picked, (probability - 1.0) * margin_slope[:, None], probability)).astype(jnp.bfloat16)
        return (carried + jnp.dot(weights, centre_unit, preferred_element_type=jnp.float32), None)
    grad_unit, _ = lax.scan(second_pass, jnp.zeros(unit_rows.shape, jnp.float32), (blocks, block_ids))
    unit_wide = unit_rows.astype(jnp.float32)
    inner_dots = lax.optimization_barrier(jnp.sum(unit_wide * grad_unit, axis=1))
    feat_grad = (grad_unit - unit_wide * inner_dots[:, None]) / length[:, None]
    return (row_loss, feat_grad)
```

```python
import math

import jax
import jax.numpy as jnp
from jax import lax
from jax.experimental import pallas as pl
from jax.experimental.pallas import tpu as pltpu
from jax.sharding import Mesh, PartitionSpec as P

logit_scale = 64.0
angle_margin = 0.5
exp2_scale = logit_scale / math.log(2.0)
vmem_limit = 56 * 1024 * 1024
lanes = 128
f32 = jnp.float32
bf16 = jnp.bfloat16


def params(**kw):
    return pltpu.CompilerParams(vmem_limit_bytes=vmem_limit, **kw)


def arc_target(target_cos):
    target_sine = jnp.sqrt(jnp.maximum(1.0 - target_cos * target_cos, 0.01))
    inside = target_cos > -math.cos(angle_margin)
    shifted = jnp.where(
        inside,
        target_cos * math.cos(angle_margin) - target_sine * math.sin(angle_margin),
        target_cos - angle_margin * math.sin(angle_margin),
    )
    margin_slope = jnp.where(
        inside, math.cos(angle_margin) + math.sin(angle_margin) * target_cos / target_sine, 1.0
    )
    return (shifted, margin_slope)


def layer_norm(values, gain_vec):
    average = jnp.mean(values, axis=-1, keepdims=True)
    centred = values - average
    variance = jnp.mean(centred * centred, axis=-1, keepdims=True)
    return centred * lax.rsqrt(variance + 1e-06) * gain_vec


def split3(value):
    hi = value.astype(bf16).astype(f32)
    mid = (value - hi).astype(bf16).astype(f32)
    return hi, mid, value - hi - mid


def ffn_kernel(tokens_ref, gain_ref, win_ref, wout_ref, out_ref, mean_ref, tok_ref):
    step = pl.program_id(0)
    block, width = tokens_ref.shape
    toks = 64
    per = block // toks
    wide = tokens_ref[...].astype(f32)
    normed = layer_norm(wide, gain_ref[...]).astype(bf16)
    pre = jnp.dot(normed, win_ref[...], preferred_element_type=f32)
    hidden = (0.5 * pre * (1.0 + lax.erf(pre * math.sqrt(0.5)))).astype(bf16).astype(f32)
    for k in range(per):
        mean_ref[pl.ds(step * per + k, 1), :] = (
            jnp.sum(hidden[k * toks : (k + 1) * toks], axis=0, keepdims=True) * (1.0 / toks)
        )
        tok_ref[pl.ds(step * per + k, 1), :] = (
            jnp.sum(wide[k * toks : (k + 1) * toks], axis=0, keepdims=True) * (0.25 / toks)
        )

    @pl.when(step == pl.num_programs(0) - 1)
    def _():
        mean = mean_ref[...]
        hi = mean.astype(bf16)
        lo = (mean - hi.astype(f32)).astype(bf16)
        wout = wout_ref[...]
        out_ref[...] = (
            jnp.dot(hi, wout, preferred_element_type=f32)
            + jnp.dot(lo, wout, preferred_element_type=f32)
            + tok_ref[...]
        )


def feed_forward(tokens, gain, weight_in, weight_out):
    rows, width = tokens.shape
    hidden = weight_in.shape[1]
    images = rows // 64
    block = 256
    return pl.pallas_call(
        ffn_kernel,
        grid=(rows // block,),
        in_specs=[
            pl.BlockSpec((block, width), lambda i: (i, 0)),
            pl.BlockSpec((1, width), lambda i: (0, 0)),
            pl.BlockSpec((width, hidden), lambda i: (0, 0)),
            pl.BlockSpec((hidden, width), lambda i: (0, 0)),
        ],
        out_specs=pl.BlockSpec((images, width), lambda i: (0, 0)),
        out_shape=jax.ShapeDtypeStruct((images, width), f32),
        scratch_shapes=[pltpu.VMEM((images, hidden), f32), pltpu.VMEM((images, width), f32)],
        compiler_params=params(),
        cost_estimate=pl.CostEstimate(
            flops=2 * rows * width * hidden, bytes_accessed=6 << 20, transcendentals=rows * hidden
        ),
        name="ffn",
    )(tokens, gain, weight_in, weight_out)


def unit_kernel(labels_ref, mine_ref, other_ref, gain_ref, send_ref, unit_ref, len_ref):
    images, width = mine_ref.shape
    pooled = mine_ref[...] + other_ref[...]
    embedding = layer_norm(pooled, gain_ref[...])
    length = jnp.sqrt(jnp.sum(embedding * embedding, axis=1, keepdims=True) + 1e-06)
    unit = (embedding / length).astype(bf16)
    row = lax.broadcasted_iota(jnp.int32, (images, lanes), 0)
    lane = lax.broadcasted_iota(jnp.int32, (images, lanes), 1)
    label = jnp.zeros((images, lanes), jnp.int32)
    for r in range(images):
        label = jnp.where(row == r, labels_ref[r], label)
    digits = jnp.where(
        lane == 0,
        label & 127,
        jnp.where(lane == 1, (label >> 7) & 127, jnp.where(lane == 2, label >> 14, 0)),
    )
    payload = jnp.concatenate([unit, digits.astype(f32).astype(bf16)], axis=1)
    for d in range(send_ref.shape[0]):
        send_ref[d] = payload
    unit_ref[...] = unit
    len_ref[...] = jnp.broadcast_to(length, (images, lanes))


def unit_rows_of(labels, mine, other, gain, homes):
    images, width = mine.shape
    return pl.pallas_call(
        unit_kernel,
        in_specs=[
            pl.BlockSpec(memory_space=pltpu.SMEM),
            pl.BlockSpec(memory_space=pltpu.VMEM),
            pl.BlockSpec(memory_space=pltpu.VMEM),
            pl.BlockSpec(memory_space=pltpu.VMEM),
        ],
        out_shape=(
            jax.ShapeDtypeStruct((homes, images, width + lanes), bf16),
            jax.ShapeDtypeStruct((images, width), bf16),
            jax.ShapeDtypeStruct((images, lanes), f32),
        ),
        compiler_params=params(),
        name="unit_rows",
    )(labels, mine, other, gain)


def centre_kernel(c_ref, after_ref, o_ref):
    wide = c_ref[...].astype(f32)
    o_ref[...] = (
        wide * lax.rsqrt(jnp.sum(wide * wide, axis=1, keepdims=True) + 1e-06)
    ).astype(bf16)


def unit_centres(centres, after):
    count, width = centres.shape
    block = 1024
    return pl.pallas_call(
        centre_kernel,
        grid=(count // block,),
        in_specs=[
            pl.BlockSpec((block, width), lambda i: (i, 0)),
            pl.BlockSpec(after.shape, lambda i: (0, 0)),
        ],
        out_specs=pl.BlockSpec((block, width), lambda i: (i, 0)),
        out_shape=jax.ShapeDtypeStruct((count, width), bf16),
        compiler_params=params(),
        cost_estimate=pl.CostEstimate(
            flops=4 * count * width, bytes_accessed=4 * count * width, transcendentals=count
        ),
        name="unit_centres",
    )(centres, after)


def digit_weights(shape, axis):
    at = lax.broadcasted_iota(jnp.int32, shape, axis)
    return jnp.where(
        at == 0, 1.0, jnp.where(at == 1, 128.0, jnp.where(at == 2, 16384.0, 0.0))
    ).astype(bf16)


def store_halves(core, width, keep_ref, send_ref, get):
    part = width // 4
    for group in range(2):
        keep_at = pl.multiple_of((2 * group + core) * part, part)
        send_at = pl.multiple_of((2 * group + 1 - core) * part, part)
        keep_ref[:, group * part : (group + 1) * part] = get(keep_at, part).astype(keep_ref.dtype)
        send_ref[:, group * part : (group + 1) * part] = get(send_at, part).astype(send_ref.dtype)


def target_kernel(where_ref, all_ref, centres_ref, keep_ref, send_ref, cos_ref, rows, found, lab, lab_s, sem, lab_sem):
    offset, core = where_ref[0], where_ref[1]
    images = all_ref.shape[0]
    count, width = centres_ref.shape
    weights = digit_weights((8, lanes), 1)
    row = lax.dot_general(
        weights, all_ref[:, width:], (((1,), (1,)), ((), ())), preferred_element_type=f32
    )
    lab[...] = row.astype(jnp.int32) - offset
    copy = pltpu.make_async_copy(lab, lab_s, lab_sem)
    copy.start()
    found[...] = jnp.zeros(found.shape, f32)
    copy.wait()

    def fetch(i):
        first = pl.multiple_of((lab_s[0, i] >> 4) << 4, 16)
        return pltpu.make_async_copy(centres_ref.at[pl.ds(first, 16), :], rows.at[i], sem)

    def local(i):
        at = lab_s[0, i]
        return jnp.logical_and(at >= 0, at < count)

    def start(i, c):
        @pl.when(local(i))
        def _():
            fetch(i).start()
        return c

    def finish(i, c):
        @pl.when(local(i))
        def _():
            fetch(i).wait()
        return c

    def take(i, c):
        @pl.when(local(i))
        def _():
            sub = lax.broadcasted_iota(jnp.int32, (16, width), 0)
            value = jnp.where(sub == (lab_s[0, i] & 15), rows[i].astype(f32), 0.0)
            found[pl.ds(i, 1), :] = jnp.sum(value, axis=0, keepdims=True)
        return c

    lax.fori_loop(0, images, start, 0, unroll=8)
    lax.fori_loop(0, images, finish, 0, unroll=8)
    lax.fori_loop(0, images, take, 0, unroll=8)
    cos = jnp.sum(found[...] * all_ref[:, :width].astype(f32), axis=1, keepdims=True)
    cos_ref[...] = jnp.broadcast_to(cos, cos_ref.shape)
    store_halves(core, width, keep_ref, send_ref, lambda at, n: found[:, pl.ds(at, n)])


def target_rows(where, gathered, centre_unit):
    images = gathered.shape[0]
    count, width = centre_unit.shape
    half = jax.ShapeDtypeStruct((images, width // 2), bf16)
    return pl.pallas_call(
        target_kernel,
        in_specs=[
            pl.BlockSpec(memory_space=pltpu.SMEM),
            pl.BlockSpec(memory_space=pltpu.VMEM),
            pl.BlockSpec(memory_space=pl.ANY),
        ],
        out_shape=(half, half, jax.ShapeDtypeStruct((images, lanes), f32)),
        scratch_shapes=[
            pltpu.VMEM((images, 16, width), bf16),
            pltpu.VMEM((images, width), f32),
            pltpu.VMEM((8, images), jnp.int32),
            pltpu.SMEM((8, images), jnp.int32),
            pltpu.SemaphoreType.DMA,
            pltpu.SemaphoreType.DMA,
        ],
        compiler_params=params(),
        cost_estimate=pl.CostEstimate(flops=1 << 20, bytes_accessed=8 << 20, transcendentals=0),
        name="target_rows",
    )(where, gathered, centre_unit)


def class_kernel(where_ref, all_ref, cos_ref, centres_ref, keep_ref, send_ref, acc, tot, lab):
    offset, core = where_ref[0], where_ref[1]
    step = pl.program_id(0)
    images = all_ref.shape[0]
    block, width = centres_ref.shape
    chunk = min(256, images)

    @pl.when(step == 0)
    def _():
        lab[...] = (
            jnp.dot(all_ref[:, width:], digit_weights((lanes, lanes), 0), preferred_element_type=f32)
        ).astype(jnp.int32) - offset
        acc[...] = jnp.zeros(acc.shape, f32)
        tot[...] = jnp.zeros(tot.shape, f32)

    base = step * block
    centres = centres_ref[...]
    for first in range(0, images, chunk):
        rows = slice(first, first + chunk)
        cosine = lax.dot_general(
            all_ref[rows, :width], centres, (((1,), (1,)), ((), ())), preferred_element_type=f32
        )
        local = lab[rows, :] - base
        lane = lax.broadcasted_iota(jnp.int32, (chunk, lanes), 1)
        parts = []
        total = tot[rows, :]
        for j in range(block // lanes):
            value = jnp.exp2(cosine[:, j * lanes : (j + 1) * lanes] * exp2_scale)
            value = jnp.where(local == lane + j * lanes, 0.0, value)
            total = total + value
            parts.append(value.astype(bf16))
        tot[rows, :] = total
        acc[rows, :] += jnp.dot(
            jnp.concatenate(parts, axis=1), centres, preferred_element_type=f32
        )

    @pl.when(step == pl.num_programs(0) - 1)
    def _():
        half = width // 2
        store_halves(core, width, keep_ref, send_ref, lambda at, n: acc[:, pl.ds(at, n)])
        total = jnp.sum(tot[...], axis=1, keepdims=True)
        inner = jnp.sum(acc[...] * all_ref[:, :width].astype(f32), axis=1, keepdims=True)
        extra = pack_extra((images, lanes), total, inner, cos_ref[...])
        keep_ref[:, half:] = extra
        send_ref[:, half:] = extra.astype(bf16)


def pack_extra(shape, total, inner, cos):
    lane = lax.broadcasted_iota(jnp.int32, shape, 1)
    out = jnp.zeros(shape, f32)
    for k, value in enumerate((total, inner, cos)):
        for j, piece in enumerate(split3(value)):
            out = jnp.where(lane == 3 * k + j, piece, out)
    return out


def unpack_extra(extra):
    values = []
    for k in range(3):
        values.append(
            extra[:, 3 * k : 3 * k + 1]
            + extra[:, 3 * k + 1 : 3 * k + 2]
            + extra[:, 3 * k + 2 : 3 * k + 3]
        )
    return values


def class_pass(where, gathered, cos, centre_unit):
    images = gathered.shape[0]
    count, width = centre_unit.shape
    block = 1024
    shape = (images, width // 2 + lanes)
    return pl.pallas_call(
        class_kernel,
        grid=(count // block,),
        in_specs=[
            pl.BlockSpec(memory_space=pltpu.SMEM),
            pl.BlockSpec(gathered.shape, lambda i: (0, 0)),
            pl.BlockSpec(cos.shape, lambda i: (0, 0)),
            pl.BlockSpec((block, width), lambda i: (i, 0)),
        ],
        out_specs=(
            pl.BlockSpec(shape, lambda i: (0, 0)),
            pl.BlockSpec(shape, lambda i: (0, 0)),
        ),
        out_shape=(jax.ShapeDtypeStruct(shape, f32), jax.ShapeDtypeStruct(shape, bf16)),
        scratch_shapes=[
            pltpu.VMEM((images, width), f32),
            pltpu.VMEM((images, lanes), f32),
            pltpu.VMEM((images, lanes), jnp.int32),
        ],
        compiler_params=params(),
        cost_estimate=pl.CostEstimate(
            flops=4 * images * count * width,
            bytes_accessed=2 * count * width,
            transcendentals=images * count,
        ),
        name="class_pass",
    )(where, gathered, cos, centre_unit)


def pair_kernel(keep_ref, got_ref, keep_row_ref, got_row_ref, out_ref):
    images = keep_ref.shape[0]
    half = keep_row_ref.shape[1]
    part = half // 2
    homes, own = out_ref.shape[0] // 2, out_ref.shape[1]
    summed = keep_ref[...] + got_ref[...].astype(f32)
    target = keep_row_ref[...] + got_row_ref[...]
    extra = pack_extra((images, lanes), *unpack_extra(summed[:, half:])).astype(bf16)
    for group in range(2):
        cols = slice(group * part, (group + 1) * part)
        at = slice(group * homes, (group + 1) * homes)
        out_ref[at, :, :part] = summed[:, cols].astype(bf16).reshape(homes, own, part)
        out_ref[at, :, part : 2 * part] = target[:, cols].reshape(homes, own, part)
        out_ref[at, :, 2 * part :] = extra.reshape(homes, own, lanes)


def pair_sum(keep, got, keep_rows, got_rows, homes):
    images = keep.shape[0]
    half = keep_rows.shape[1]
    return pl.pallas_call(
        pair_kernel,
        out_shape=jax.ShapeDtypeStruct((2 * homes, images // homes, half + lanes), bf16),
        compiler_params=params(),
        name="pair_sum",
    )(keep, got, keep_rows, got_rows)


def home_kernel(where_ref, got_ref, unit_ref, len_ref, loss_ref, grad_ref):
    column = where_ref[2]
    part = grad_ref.shape[1]
    summed = jnp.sum(got_ref[...].astype(f32), axis=0)
    gradient = summed[:, :part]
    target = summed[:, part : 2 * part]
    rest, inner, cos = unpack_extra(summed[:, 2 * part :])
    shifted, slope = arc_target(cos)
    own = jnp.exp(logit_scale * shifted)
    total = rest + own
    loss_ref[...] = jnp.broadcast_to(jnp.log(total) - logit_scale * shifted, loss_ref.shape)
    weight = (logit_scale * ((own / total - 1.0) * slope)).astype(bf16).astype(f32)
    scale = logit_scale / total
    dots = inner * scale + weight * cos
    unit = unit_ref[:, pl.ds(pl.multiple_of(column * part, part), part)].astype(f32)
    grad_ref[...] = (gradient * scale + weight * target - unit * dots) / len_ref[:, :1]


def home(where, got, unit, length):
    images = unit.shape[0]
    part = unit.shape[1] // 4
    return pl.pallas_call(
        home_kernel,
        in_specs=[
            pl.BlockSpec(memory_space=pltpu.SMEM),
            pl.BlockSpec(memory_space=pltpu.VMEM),
            pl.BlockSpec(memory_space=pltpu.VMEM),
            pl.BlockSpec(memory_space=pltpu.VMEM),
        ],
        out_shape=(
            jax.ShapeDtypeStruct((images, lanes), f32),
            jax.ShapeDtypeStruct((images, part), f32),
        ),
        compiler_params=params(),
        name="home",
    )(where, got, unit, length)


swap = [(0, 1), (1, 0)]


def shards(tokens, norm_gain, weight_in, weight_out, final_gain, centres, labels):
    images, tok_count, width = tokens.shape
    count = centres.shape[0]
    homes = lax.axis_size("dp")
    core = lax.axis_index("core")
    column = lax.axis_index("z_hi") * 2 + core
    offset = (column * homes + lax.axis_index("dp")) * count
    where = jnp.stack([offset, core, column]).astype(jnp.int32)

    partial = feed_forward(
        tokens.reshape(-1, width), norm_gain[None], weight_in, weight_out
    )
    partial = partial + lax.ppermute(partial, "core", swap)
    other = lax.ppermute(partial, "z_hi", swap)
    send, unit, length = unit_rows_of(labels, partial, other, final_gain[None], homes)
    gathered = lax.all_to_all(send, "dp", 0, 0, tiled=True).reshape(homes * images, -1)
    centre_unit = unit_centres(centres, length)
    keep_rows, send_rows, cos = target_rows(where, gathered, centre_unit)
    got_rows = lax.ppermute(send_rows, "core", swap)
    keep, give = class_pass(where, gathered, cos, centre_unit)
    got = lax.ppermute(give, "core", swap)
    paired = pair_sum(keep, got, keep_rows, got_rows, homes)
    arrived = lax.all_to_all(paired, ("z_hi", "dp"), 0, 0, tiled=True)
    loss, grad = home(where, arrived, unit, length)
    return (loss[:, 0], grad)


def solution(mesh):
    fine = Mesh(mesh.devices.reshape(2, 2, -1), ("z_hi", "core", "dp"))
    mp = ("z_hi", "core")
    return jax.shard_map(
        shards,
        mesh=fine,
        in_specs=(
            P("dp", None, None),
            P(),
            P(None, mp),
            P(mp, None),
            P(),
            P((*mp, "dp"), None),
            P("dp"),
        ),
        out_specs=(P("dp"), P("dp", mp)),
        check_vma=False,
    )
```

```python
import math

import jax
import jax.numpy as jnp
from jax import lax
from jax.experimental import pallas as pl
from jax.experimental.pallas import tpu as pltpu
from jax.sharding import Mesh, PartitionSpec as P

logit_scale = 64.0
angle_margin = 0.5
exp2_scale = logit_scale / math.log(2.0)
lanes = 128
digits = 3
pieces = 8
f32 = jnp.float32
bf16 = jnp.bfloat16


def params(mebibytes):
    return pltpu.CompilerParams(vmem_limit_bytes=mebibytes * 1024 * 1024)


def arc_target(target_cos):
    target_sine = jnp.sqrt(jnp.maximum(1.0 - target_cos * target_cos, 0.01))
    inside = target_cos > -math.cos(angle_margin)
    shifted = jnp.where(
        inside,
        target_cos * math.cos(angle_margin) - target_sine * math.sin(angle_margin),
        target_cos - angle_margin * math.sin(angle_margin),
    )
    margin_slope = jnp.where(
        inside, math.cos(angle_margin) + math.sin(angle_margin) * target_cos / target_sine, 1.0
    )
    return (shifted, margin_slope)


def layer_norm(values, gain_vec):
    average = jnp.mean(values, axis=-1, keepdims=True)
    centred = values - average
    variance = jnp.mean(centred * centred, axis=-1, keepdims=True)
    return centred * lax.rsqrt(variance + 1e-06) * gain_vec


def split3(value):
    hi = value.astype(bf16).astype(f32)
    mid = (value - hi).astype(bf16).astype(f32)
    return hi, mid, value - hi - mid


def ffn_kernel(tokens_ref, gain_ref, win_ref, wout_ref, out_ref, mean_ref, tok_ref):
    step = pl.program_id(0)
    block, width = tokens_ref.shape
    toks = 64
    per = block // toks
    wide = tokens_ref[...].astype(f32)
    normed = layer_norm(wide, gain_ref[...]).astype(bf16)
    pre = jnp.dot(normed, win_ref[...], preferred_element_type=f32)
    hidden = (0.5 * pre * (1.0 + lax.erf(pre * math.sqrt(0.5)))).astype(bf16).astype(f32)
    for k in range(per):
        mean_ref[pl.ds(step * per + k, 1), :] = (
            jnp.sum(hidden[k * toks : (k + 1) * toks], axis=0, keepdims=True) * (1.0 / toks)
        )
        tok_ref[pl.ds(step * per + k, 1), :] = (
            jnp.sum(wide[k * toks : (k + 1) * toks], axis=0, keepdims=True) * (0.25 / toks)
        )

    @pl.when(step == pl.num_programs(0) - 1)
    def _():
        mean = mean_ref[...]
        hi = mean.astype(bf16)
        lo = (mean - hi.astype(f32)).astype(bf16)
        both = jnp.dot(
            jnp.concatenate([hi, lo], axis=0), wout_ref[...], preferred_element_type=f32
        )
        images = mean.shape[0]
        out_ref[...] = both[:images] + both[images:] + tok_ref[...]


def feed_forward(tokens, gain, weight_in, weight_out):
    rows, width = tokens.shape
    hidden = weight_in.shape[1]
    images = rows // 64
    block = 256
    return pl.pallas_call(
        ffn_kernel,
        grid=(rows // block,),
        in_specs=[
            pl.BlockSpec((block, width), lambda i: (i, 0)),
            pl.BlockSpec((1, width), lambda i: (0, 0)),
            pl.BlockSpec((width, hidden), lambda i: (0, 0)),
            pl.BlockSpec((hidden, width), lambda i: (0, 0)),
        ],
        out_specs=pl.BlockSpec((images, width), lambda i: (0, 0)),
        out_shape=jax.ShapeDtypeStruct((images, width), f32),
        scratch_shapes=[pltpu.VMEM((images, hidden), f32), pltpu.VMEM((images, width), f32)],
        compiler_params=params(56),
        cost_estimate=pl.CostEstimate(
            flops=2 * rows * width * hidden, bytes_accessed=6 << 20, transcendentals=rows * hidden
        ),
        name="ffn",
    )(tokens, gain, weight_in, weight_out)


def unit_kernel(where_ref, labels_ref, mine_ref, other_ref, gain_ref, send_ref, unit_ref, len_ref):
    images, width = mine_ref.shape
    pooled = mine_ref[...] + other_ref[...]
    embedding = layer_norm(pooled, gain_ref[...])
    length = jnp.sqrt(jnp.sum(embedding * embedding, axis=1, keepdims=True) + 1e-06)
    unit = (embedding / length).astype(bf16).astype(f32)
    half = images // 2
    row = lax.broadcasted_iota(jnp.int32, (half, lanes), 0)
    lane = lax.broadcasted_iota(jnp.int32, (half, lanes), 1)
    label = jnp.zeros((half, lanes), jnp.int32)
    for h in range(2):
        for r in range(half):
            here = jnp.logical_and(row == r, lane // digits == h)
            label = jnp.where(here, labels_ref[h * half + r], label)
    place = lane % digits
    coded = jnp.where(
        place == 0, label & 127, jnp.where(place == 1, (label >> 7) & 127, label >> 14)
    )
    payload = jnp.concatenate([unit[:half], unit[half:], coded.astype(f32)], axis=1)
    payload = jnp.concatenate([payload, payload], axis=0).astype(bf16)
    for d in range(send_ref.shape[0] // images):
        send_ref[d * images : (d + 1) * images, :] = payload
    unit_ref[...] = unit
    len_ref[...] = jnp.broadcast_to(length, (images, lanes))


def unit_rows_of(where, labels, mine, other, gain, homes):
    images, width = mine.shape
    return pl.pallas_call(
        unit_kernel,
        in_specs=[
            pl.BlockSpec(memory_space=pltpu.SMEM),
            pl.BlockSpec(memory_space=pltpu.SMEM),
            pl.BlockSpec(memory_space=pltpu.VMEM),
            pl.BlockSpec(memory_space=pltpu.VMEM),
            pl.BlockSpec(memory_space=pltpu.VMEM),
        ],
        out_shape=(
            jax.ShapeDtypeStruct((homes * images // 2, 2 * width + lanes), bf16),
            jax.ShapeDtypeStruct((images, width), f32),
            jax.ShapeDtypeStruct((images, lanes), f32),
        ),
        compiler_params=params(8),
        name="unit_rows",
    )(where, labels, mine, other, gain)


def digit_weights(shape, axis, h):
    at = lax.broadcasted_iota(jnp.int32, shape, axis) - h * digits
    return jnp.where(
        at == 0, 1.0, jnp.where(at == 1, 128.0, jnp.where(at == 2, 16384.0, 0.0))
    ).astype(bf16)


group_size = 16


def class_kernel(
    where_ref,
    all_ref,
    centres_ref,
    keep_ref,
    keep_row_ref,
    send_ref,
    held,
    unit,
    acc,
    tot,
    cos_row,
    lab,
    lab_s,
    found_s,
    lab_sem,
    sems,
):
    offset, core = where_ref[0], where_ref[1]
    rows = all_ref.shape[0]
    images = 2 * rows
    count, width = centres_ref.shape
    block = count // pieces
    half, part = width // 2, width // 4
    groups = images // group_size

    def fetch(i):
        at = pl.ds(pl.multiple_of(i * block, block), block)
        return pltpu.make_async_copy(centres_ref.at[at, :], held.at[at, :], sems.at[i])

    for i in range(pieces):
        fetch(i).start()

    coded = all_ref[:, 2 * width :]
    turned = (((1,), (1,)), ((), ()))
    for h in range(2):
        unit[h * rows : (h + 1) * rows, :] = all_ref[:, h * width : (h + 1) * width]
        lab[:, h * rows : (h + 1) * rows] = lax.dot_general(
            digit_weights((8, lanes), 1, h), coded, turned, preferred_element_type=f32
        ).astype(jnp.int32) - offset
    row = lab[:, :images]
    member = lax.broadcasted_iota(jnp.int32, (images, lanes), 0) // group_size
    member = (member == lax.broadcasted_iota(jnp.int32, (images, lanes), 1)).astype(bf16)
    inside = jnp.logical_and(row >= 0, row < count).astype(f32).astype(bf16)
    lab[:, images:] = jnp.dot(inside, member, preferred_element_type=f32).astype(jnp.int32)
    copy = pltpu.make_async_copy(lab, lab_s, lab_sem)
    copy.start()
    local = jnp.concatenate(
        [
            jnp.dot(coded, digit_weights((lanes, lanes), 0, h), preferred_element_type=f32)
            for h in range(2)
        ],
        axis=0,
    ).astype(jnp.int32) - offset
    acc[...] = jnp.zeros(acc.shape, f32)
    tot[...] = jnp.zeros(tot.shape, f32)
    cos_row[...] = jnp.zeros(cos_row.shape, f32)
    keep_row_ref[...] = jnp.zeros(keep_row_ref.shape, bf16)
    send_ref[:, width : 2 * width] = jnp.zeros((rows, width), bf16)
    copy.wait()
    found_s[images] = 0

    def look(g, c):
        @pl.when(lab_s[0, images + g] > 0)
        def _():
            for k in range(group_size):
                i = g * group_size + k
                at = lab_s[0, i]

                @pl.when(jnp.logical_and(at >= 0, at < count))
                def _():
                    n = found_s[images]
                    found_s[n] = i
                    found_s[images] = n + 1

        return c

    lax.fori_loop(0, groups, look, 0)

    diagonal = lax.broadcasted_iota(jnp.int32, (lanes, lanes), 0) == lax.broadcasted_iota(
        jnp.int32, (lanes, lanes), 1
    )

    def step(t, c):
        base = pl.multiple_of(t * block, block)
        fetch(t).wait()
        centres = held[pl.ds(base, block), :]
        cosine = lax.dot_general(unit[...], centres, turned, preferred_element_type=f32)
        lane = lax.broadcasted_iota(jnp.int32, (images, lanes), 1) + base
        parts = []
        total = tot[...]
        for j in range(block // lanes):
            wide = held[pl.ds(base + j * lanes, lanes), :].astype(f32)
            square = jnp.sum(wide * wide, axis=1, keepdims=True)
            square = jnp.sum(jnp.where(diagonal, square, 0.0), axis=0, keepdims=True)
            inverse = lax.rsqrt(square + 1e-06)
            value = jnp.exp2(cosine[:, j * lanes : (j + 1) * lanes] * (inverse * exp2_scale))
            value = jnp.where(local == lane + j * lanes, 0.0, value)
            total = total + value
            parts.append((value * inverse).astype(bf16))
        tot[...] = total
        acc[...] += jnp.dot(jnp.concatenate(parts, axis=1), centres, preferred_element_type=f32)
        return c

    lax.fori_loop(0, pieces, step, 0)

    sub = lax.broadcasted_iota(jnp.int32, (16, width), 0)

    def take(k, c):
        i = found_s[k]
        at = lab_s[0, i]
        raw = held[pl.ds(pl.multiple_of((at >> 4) << 4, 16), 16), :].astype(f32)
        raw = jnp.sum(jnp.where(sub == (at & 15), raw, 0.0), axis=0, keepdims=True)
        found = raw * lax.rsqrt(jnp.sum(raw * raw, axis=1, keepdims=True) + 1e-06)
        found = found.astype(bf16).astype(f32)
        mine = sub == (i & 15)
        first = pl.multiple_of((i >> 4) << 4, 16)
        image = unit[pl.ds(first, 16), :].astype(f32)
        cos = jnp.sum(jnp.where(mine, image * found, 0.0), axis=1, keepdims=True)
        cos_row[pl.ds(first, 16), :] = jnp.where(
            mine[:, :lanes], cos, cos_row[pl.ds(first, 16), :]
        )
        even = jnp.concatenate([found[:, :part], found[:, half : half + part]], axis=1)
        odd = jnp.concatenate([found[:, part:half], found[:, half + part :]], axis=1)
        kept = jnp.where(core == 0, even, odd)
        sent = jnp.where(core == 0, odd, even)
        for h in range(2):

            @pl.when((i >= rows) == (h == 1))
            def _():
                here = pl.ds(pl.multiple_of(first - h * rows, 16), 16)
                for ref, start, value in ((keep_row_ref, 0, kept), (send_ref, width, sent)):
                    cols = slice(start + h * half, start + (h + 1) * half)
                    ref[here, cols] = jnp.where(
                        mine[:, :half], value, ref[here, cols].astype(f32)
                    ).astype(bf16)

        return c

    lax.fori_loop(0, found_s[images], take, 0)

    extras = []
    for h in range(2):
        at = slice(h * rows, (h + 1) * rows)
        for group in range(2):
            cols = slice(h * half + group * part, h * half + (group + 1) * part)
            keep_at = pl.multiple_of((2 * group + core) * part, part)
            send_at = pl.multiple_of((2 * group + 1 - core) * part, part)
            keep_ref[:, cols] = acc[at, pl.ds(keep_at, part)]
            send_ref[:, cols] = acc[at, pl.ds(send_at, part)].astype(bf16)
        total = jnp.sum(tot[at, :], axis=1, keepdims=True)
        inner = jnp.sum(acc[at, :] * unit[at, :].astype(f32), axis=1, keepdims=True)
        extras.append((total, inner, cos_row[at, :1]))
    extra = pack_extra(extras)
    keep_ref[:, width:] = extra
    send_ref[:, 2 * width :] = extra.astype(bf16)


def pack_extra(halves):
    shape = (halves[0][0].shape[0], lanes)
    lane = lax.broadcasted_iota(jnp.int32, shape, 1)
    out = jnp.zeros(shape, f32)
    k = 0
    for values in halves:
        for value in values:
            for piece in split3(value):
                out = jnp.where(lane == k, piece, out)
                k += 1
    return out


def unpack_extra(extra):
    halves = []
    for h in range(2):
        values = []
        for k in range(3 * h, 3 * h + 3):
            values.append(
                extra[:, 3 * k : 3 * k + 1]
                + extra[:, 3 * k + 1 : 3 * k + 2]
                + extra[:, 3 * k + 2 : 3 * k + 3]
            )
        halves.append(values)
    return halves


def class_pass(where, gathered, centres):
    rows = gathered.shape[0]
    images = 2 * rows
    count, width = centres.shape
    return pl.pallas_call(
        class_kernel,
        in_specs=[
            pl.BlockSpec(memory_space=pltpu.SMEM),
            pl.BlockSpec(memory_space=pltpu.VMEM),
            pl.BlockSpec(memory_space=pltpu.HBM),
        ],
        out_shape=(
            jax.ShapeDtypeStruct((rows, width + lanes), f32),
            jax.ShapeDtypeStruct((rows, width), bf16),
            jax.ShapeDtypeStruct((rows, 2 * width + lanes), bf16),
        ),
        scratch_shapes=[
            pltpu.VMEM((count, width), bf16),
            pltpu.VMEM((images, width), bf16),
            pltpu.VMEM((images, width), f32),
            pltpu.VMEM((images, lanes), f32),
            pltpu.VMEM((images, lanes), f32),
            pltpu.VMEM((8, images + lanes), jnp.int32),
            pltpu.SMEM((8, images + lanes), jnp.int32),
            pltpu.SMEM((images + 1,), jnp.int32),
            pltpu.SemaphoreType.DMA,
            pltpu.SemaphoreType.DMA((pieces,)),
        ],
        compiler_params=params(48),
        cost_estimate=pl.CostEstimate(
            flops=4 * images * count * width,
            bytes_accessed=2 * count * width,
            transcendentals=images * count,
        ),
        name="class_pass",
    )(where, gathered, centres)


def pair_kernel(keep_ref, keep_row_ref, got_ref, out_ref):
    rows, width = keep_row_ref.shape
    half, part = width // 2, width // 4
    summed = keep_ref[...] + jnp.concatenate(
        [got_ref[:, :width].astype(f32), got_ref[:, 2 * width :].astype(f32)], axis=1
    )
    target = keep_row_ref[...] + got_ref[:, width : 2 * width]
    extra = pack_extra(unpack_extra(summed[:, width:])).astype(bf16)
    for group in range(2):
        at = slice(group * rows, (group + 1) * rows)
        for h in range(2):
            cols = slice(h * half + group * part, h * half + (group + 1) * part)
            out_ref[at, h * part : (h + 1) * part] = summed[:, cols].astype(bf16)
            out_ref[at, half + h * part : half + (h + 1) * part] = target[:, cols]
        out_ref[at, width:] = extra


def pair_sum(keep, keep_rows, got):
    rows, width = keep_rows.shape
    return pl.pallas_call(
        pair_kernel,
        out_shape=jax.ShapeDtypeStruct((2 * rows, width + lanes), bf16),
        compiler_params=params(12),
        name="pair_sum",
    )(keep, keep_rows, got)


def home_kernel(where_ref, got_ref, unit_ref, len_ref, loss_ref, grad_ref):
    column = where_ref[2]
    images, part = grad_ref.shape
    half = images // 2
    summed = jnp.zeros((images, got_ref.shape[1]), f32)
    for k in range(0, got_ref.shape[0], images):
        summed = summed + got_ref[k : k + images, :].astype(f32)
    summed = summed[:half] + summed[half:]
    row = lax.broadcasted_iota(jnp.int32, (half, images), 0)
    lane = lax.broadcasted_iota(jnp.int32, (half, images), 1)
    loss_row = jnp.zeros((1, images), f32)
    for h, (rest, inner, cos) in enumerate(unpack_extra(summed[:, 4 * part :])):
        at = slice(h * half, (h + 1) * half)
        gradient = summed[:, h * part : (h + 1) * part]
        target = summed[:, (2 + h) * part : (3 + h) * part]
        shifted, slope = arc_target(cos)
        own = jnp.exp(logit_scale * shifted)
        total = rest + own
        loss = jnp.log(total) - logit_scale * shifted
        loss_row += jnp.sum(jnp.where(lane == row + h * half, loss, 0.0), axis=0, keepdims=True)
        weight = (logit_scale * ((own / total - 1.0) * slope)).astype(bf16).astype(f32)
        scale = logit_scale / total
        dots = inner * scale + weight * cos
        unit = unit_ref[at, pl.ds(pl.multiple_of(column * part, part), part)]
        grad_ref[at, :] = (gradient * scale + weight * target - unit * dots) / len_ref[at, :1]
    loss_ref[...] = loss_row


def home(where, got, unit, length):
    images = unit.shape[0]
    part = unit.shape[1] // 4
    return pl.pallas_call(
        home_kernel,
        in_specs=[
            pl.BlockSpec(memory_space=pltpu.SMEM),
            pl.BlockSpec(memory_space=pltpu.VMEM),
            pl.BlockSpec(memory_space=pltpu.VMEM),
            pl.BlockSpec(memory_space=pltpu.VMEM),
        ],
        out_shape=(
            jax.ShapeDtypeStruct((1, images), f32),
            jax.ShapeDtypeStruct((images, part), f32),
        ),
        compiler_params=params(12),
        name="home",
    )(where, got, unit, length)


swap = [(0, 1), (1, 0)]


def shards(tokens, norm_gain, weight_in, weight_out, final_gain, centres, labels):
    images, tok_count, width = tokens.shape
    count = centres.shape[0]
    homes = lax.axis_size("dp")
    core = lax.axis_index("core")
    column = lax.axis_index("z_hi") * 2 + core
    offset = (column * homes + lax.axis_index("dp")) * count
    where = jnp.stack([offset, core, column]).astype(jnp.int32)

    partial = feed_forward(
        tokens.reshape(-1, width), norm_gain[None], weight_in, weight_out
    )
    partial = partial + lax.ppermute(partial, "core", swap)
    other = lax.ppermute(partial, "z_hi", swap)
    send, unit, length = unit_rows_of(where, labels, partial, other, final_gain[None], homes)
    gathered = lax.all_to_all(send, "dp", 0, 0, tiled=True)
    keep, keep_rows, give = class_pass(where, gathered, centres)
    got = lax.ppermute(give, "core", swap)
    paired = pair_sum(keep, keep_rows, got)
    arrived = lax.all_to_all(paired, ("z_hi", "dp"), 0, 0, tiled=True)
    loss, grad = home(where, arrived, unit, length)
    return (loss[0], grad)


def solution(mesh):
    fine = Mesh(mesh.devices.reshape(2, 2, -1), ("z_hi", "core", "dp"))
    mp = ("z_hi", "core")
    return jax.shard_map(
        shards,
        mesh=fine,
        in_specs=(
            P("dp", None, None),
            P(),
            P(None, mp),
            P(mp, None),
            P(),
            P((*mp, "dp"), None),
            P("dp"),
        ),
        out_specs=(P("dp"), P("dp", mp)),
        check_vma=False,
    )
```

```python
import math

import jax
import jax.numpy as jnp
from jax import lax
from jax.experimental import pallas as pl
from jax.experimental.pallas import tpu as pltpu
from jax.sharding import Mesh, PartitionSpec as P

logit_scale = 64.0
angle_margin = 0.5
exp2_scale = logit_scale / math.log(2.0)
lanes = 128
digits = 3
pieces = 8
f32 = jnp.float32
bf16 = jnp.bfloat16


def params(mebibytes):
    return pltpu.CompilerParams(vmem_limit_bytes=mebibytes * 1024 * 1024)


def arc_target(target_cos):
    target_sine = jnp.sqrt(jnp.maximum(1.0 - target_cos * target_cos, 0.01))
    inside = target_cos > -math.cos(angle_margin)
    shifted = jnp.where(
        inside,
        target_cos * math.cos(angle_margin) - target_sine * math.sin(angle_margin),
        target_cos - angle_margin * math.sin(angle_margin),
    )
    margin_slope = jnp.where(
        inside, math.cos(angle_margin) + math.sin(angle_margin) * target_cos / target_sine, 1.0
    )
    return (shifted, margin_slope)


def layer_norm(values, gain_vec):
    average = jnp.mean(values, axis=-1, keepdims=True)
    centred = values - average
    variance = jnp.mean(centred * centred, axis=-1, keepdims=True)
    return centred * lax.rsqrt(variance + 1e-06) * gain_vec


def split3(value):
    hi = value.astype(bf16).astype(f32)
    mid = (value - hi).astype(bf16).astype(f32)
    return hi, mid, value - hi - mid


toks = 64


def ffn_kernel(tokens_ref, gain_ref, win_ref, wout_hbm, out_ref, mean_ref, tok_ref, wout, sem):
    step = pl.program_id(0)
    block, width = tokens_ref.shape
    sub = 256
    per = sub // toks
    fetch = pltpu.make_async_copy(wout_hbm, wout, sem)

    @pl.when(step == 0)
    def _():
        fetch.start()

    image = lax.broadcasted_iota(jnp.int32, (8, sub), 0)
    member = (lax.broadcasted_iota(jnp.int32, (8, sub), 1) // toks == image).astype(f32).astype(bf16)
    for k in range(block // sub):
        rows = tokens_ref[k * sub : (k + 1) * sub, :]
        normed = layer_norm(rows.astype(f32), gain_ref[...]).astype(bf16)
        pre = jnp.dot(normed, win_ref[...], preferred_element_type=f32)
        hidden = (0.5 * pre * (1.0 + lax.erf(pre * math.sqrt(0.5)))).astype(bf16)
        mean = jnp.dot(member, hidden, preferred_element_type=f32) * (1.0 / toks)
        tok = jnp.dot(member, rows, preferred_element_type=f32) * (0.25 / toks)
        for q in range(per):
            at = pl.ds(step * (block // toks) + k * per + q, 1)
            mean_ref[at, :] = mean[q : q + 1]
            tok_ref[at, :] = tok[q : q + 1]

    @pl.when(step == pl.num_programs(0) - 1)
    def _():
        fetch.wait()
        mean = mean_ref[...]
        hi = mean.astype(bf16)
        lo = (mean - hi.astype(f32)).astype(bf16)
        both = jnp.dot(jnp.concatenate([hi, lo], axis=0), wout[...], preferred_element_type=f32)
        images = mean.shape[0]
        out_ref[...] = both[:images] + both[images:] + tok_ref[...]


def feed_forward(tokens, gain, weight_in, weight_out):
    rows, width = tokens.shape
    hidden = weight_in.shape[1]
    images = rows // toks
    block = 512
    return pl.pallas_call(
        ffn_kernel,
        grid=(rows // block,),
        in_specs=[
            pl.BlockSpec((block, width), lambda i: (i, 0)),
            pl.BlockSpec((1, width), lambda i: (0, 0)),
            pl.BlockSpec((width, hidden), lambda i: (0, 0)),
            pl.BlockSpec(memory_space=pltpu.HBM),
        ],
        out_specs=pl.BlockSpec((images, width), lambda i: (0, 0)),
        out_shape=pltpu.VMEM((images, width), f32),
        scratch_shapes=[
            pltpu.VMEM((images, hidden), f32),
            pltpu.VMEM((images, width), f32),
            pltpu.VMEM((hidden, width), bf16),
            pltpu.SemaphoreType.DMA,
        ],
        compiler_params=params(58),
        cost_estimate=pl.CostEstimate(
            flops=2 * rows * width * hidden, bytes_accessed=6 << 20, transcendentals=rows * hidden
        ),
        name="ffn",
    )(tokens, gain, weight_in, weight_out)


def unit_kernel(where_ref, labels_ref, mine_ref, other_ref, gain_ref, send_ref, unit_ref, len_ref):
    images, width = mine_ref.shape
    pooled = mine_ref[...] + other_ref[...]
    embedding = layer_norm(pooled, gain_ref[...])
    length = jnp.sqrt(jnp.sum(embedding * embedding, axis=1, keepdims=True) + 1e-06)
    unit = (embedding / length).astype(bf16).astype(f32)
    half = images // 2
    row = lax.broadcasted_iota(jnp.int32, (half, lanes), 0)
    lane = lax.broadcasted_iota(jnp.int32, (half, lanes), 1)
    label = jnp.zeros((half, lanes), jnp.int32)
    for h in range(2):
        for r in range(half):
            here = jnp.logical_and(row == r, lane // digits == h)
            label = jnp.where(here, labels_ref[h * half + r], label)
    place = lane % digits
    coded = jnp.where(
        place == 0, label & 127, jnp.where(place == 1, (label >> 7) & 127, label >> 14)
    )
    payload = jnp.concatenate([unit[:half], unit[half:], coded.astype(f32)], axis=1)
    payload = jnp.concatenate([payload, payload], axis=0).astype(bf16)
    for d in range(send_ref.shape[0] // images):
        send_ref[d * images : (d + 1) * images, :] = payload
    unit_ref[...] = unit
    len_ref[...] = jnp.broadcast_to(length, (images, lanes))


def unit_rows_of(where, labels, mine, other, gain, homes):
    images, width = mine.shape
    return pl.pallas_call(
        unit_kernel,
        in_specs=[
            pl.BlockSpec(memory_space=pltpu.SMEM),
            pl.BlockSpec(memory_space=pltpu.SMEM),
            pl.BlockSpec(memory_space=pltpu.VMEM),
            pl.BlockSpec(memory_space=pltpu.VMEM),
            pl.BlockSpec(memory_space=pltpu.VMEM),
        ],
        out_shape=(
            pltpu.VMEM((homes * images // 2, 2 * width + lanes), bf16),
            jax.ShapeDtypeStruct((images, width), f32),
            jax.ShapeDtypeStruct((images, lanes), f32),
        ),
        compiler_params=params(8),
        name="unit_rows",
    )(where, labels, mine, other, gain)


def digit_weights(shape, axis, h):
    at = lax.broadcasted_iota(jnp.int32, shape, axis) - h * digits
    return jnp.where(
        at == 0, 1.0, jnp.where(at == 1, 128.0, jnp.where(at == 2, 16384.0, 0.0))
    ).astype(bf16)


group_size = 16


def class_kernel(
    where_ref,
    all_ref,
    centres_ref,
    keep_ref,
    keep_row_ref,
    send_ref,
    held,
    unit,
    acc,
    tot,
    cos_row,
    lab,
    lab_s,
    found_s,
    lab_sem,
    sems,
):
    offset, core = where_ref[0], where_ref[1]
    rows = all_ref.shape[0]
    images = 2 * rows
    count, width = centres_ref.shape
    block = count // pieces
    half, part = width // 2, width // 4
    groups = images // group_size

    def fetch(i):
        at = pl.ds(pl.multiple_of(i * block, block), block)
        return pltpu.make_async_copy(centres_ref.at[at, :], held.at[at, :], sems.at[i])

    for i in range(2):
        fetch(i).start()

    coded = all_ref[:, 2 * width :]
    turned = (((1,), (1,)), ((), ()))
    for h in range(2):
        unit[h * rows : (h + 1) * rows, :] = all_ref[:, h * width : (h + 1) * width]
        lab[:, h * rows : (h + 1) * rows] = lax.dot_general(
            digit_weights((8, lanes), 1, h), coded, turned, preferred_element_type=f32
        ).astype(jnp.int32) - offset
    row = lab[:, :images]
    member = lax.broadcasted_iota(jnp.int32, (images, lanes), 0) // group_size
    member = (member == lax.broadcasted_iota(jnp.int32, (images, lanes), 1)).astype(bf16)
    inside = jnp.logical_and(row >= 0, row < count).astype(f32).astype(bf16)
    lab[:, images:] = jnp.dot(inside, member, preferred_element_type=f32).astype(jnp.int32)
    copy = pltpu.make_async_copy(lab, lab_s, lab_sem)
    copy.start()
    local = jnp.concatenate(
        [
            jnp.dot(coded, digit_weights((lanes, lanes), 0, h), preferred_element_type=f32)
            for h in range(2)
        ],
        axis=0,
    ).astype(jnp.int32) - offset
    acc[...] = jnp.zeros(acc.shape, f32)
    tot[...] = jnp.zeros(tot.shape, f32)
    cos_row[...] = jnp.zeros(cos_row.shape, f32)
    keep_row_ref[...] = jnp.zeros(keep_row_ref.shape, bf16)
    send_ref[:, width : 2 * width] = jnp.zeros((rows, width), bf16)
    copy.wait()
    found_s[images] = 0

    def look(g, c):
        @pl.when(lab_s[0, images + g] > 0)
        def _():
            for k in range(group_size):
                i = g * group_size + k
                at = lab_s[0, i]

                @pl.when(jnp.logical_and(at >= 0, at < count))
                def _():
                    n = found_s[images]
                    found_s[n] = i
                    found_s[images] = n + 1

        return c

    lax.fori_loop(0, groups, look, 0)

    diagonal = lax.broadcasted_iota(jnp.int32, (lanes, lanes), 0) == lax.broadcasted_iota(
        jnp.int32, (lanes, lanes), 1
    )

    def step(t, c):
        base = pl.multiple_of(t * block, block)
        fetch(t).wait()

        @pl.when(t + 2 < pieces)
        def _():
            fetch(t + 2).start()

        centres = held[pl.ds(base, block), :]
        cosine = lax.dot_general(unit[...], centres, turned, preferred_element_type=f32)
        lane = lax.broadcasted_iota(jnp.int32, (images, lanes), 1) + base
        parts = []
        total = tot[...]
        for j in range(block // lanes):
            wide = held[pl.ds(base + j * lanes, lanes), :].astype(f32)
            square = jnp.sum(wide * wide, axis=1, keepdims=True)
            square = jnp.sum(jnp.where(diagonal, square, 0.0), axis=0, keepdims=True)
            inverse = lax.rsqrt(square + 1e-06)
            value = jnp.exp2(cosine[:, j * lanes : (j + 1) * lanes] * (inverse * exp2_scale))
            value = jnp.where(local == lane + j * lanes, 0.0, value)
            total = total + value
            parts.append((value * inverse).astype(bf16))
        tot[...] = total
        acc[...] += jnp.dot(jnp.concatenate(parts, axis=1), centres, preferred_element_type=f32)
        return c

    lax.fori_loop(0, pieces, step, 0)

    sub = lax.broadcasted_iota(jnp.int32, (16, width), 0)

    def take(k, c):
        i = found_s[k]
        at = lab_s[0, i]
        raw = held[pl.ds(pl.multiple_of((at >> 4) << 4, 16), 16), :].astype(f32)
        raw = jnp.sum(jnp.where(sub == (at & 15), raw, 0.0), axis=0, keepdims=True)
        found = raw * lax.rsqrt(jnp.sum(raw * raw, axis=1, keepdims=True) + 1e-06)
        found = found.astype(bf16).astype(f32)
        mine = sub == (i & 15)
        first = pl.multiple_of((i >> 4) << 4, 16)
        image = unit[pl.ds(first, 16), :].astype(f32)
        cos = jnp.sum(jnp.where(mine, image * found, 0.0), axis=1, keepdims=True)
        cos_row[pl.ds(first, 16), :] = jnp.where(
            mine[:, :lanes], cos, cos_row[pl.ds(first, 16), :]
        )
        even = jnp.concatenate([found[:, :part], found[:, half : half + part]], axis=1)
        odd = jnp.concatenate([found[:, part:half], found[:, half + part :]], axis=1)
        kept = jnp.where(core == 0, even, odd)
        sent = jnp.where(core == 0, odd, even)
        for h in range(2):

            @pl.when((i >= rows) == (h == 1))
            def _():
                here = pl.ds(pl.multiple_of(first - h * rows, 16), 16)
                for ref, start, value in ((keep_row_ref, 0, kept), (send_ref, width, sent)):
                    cols = slice(start + h * half, start + (h + 1) * half)
                    ref[here, cols] = jnp.where(
                        mine[:, :half], value, ref[here, cols].astype(f32)
                    ).astype(bf16)

        return c

    lax.fori_loop(0, found_s[images], take, 0)

    extras = []
    for h in range(2):
        at = slice(h * rows, (h + 1) * rows)
        for group in range(2):
            cols = slice(h * half + group * part, h * half + (group + 1) * part)
            keep_at = pl.multiple_of((2 * group + core) * part, part)
            send_at = pl.multiple_of((2 * group + 1 - core) * part, part)
            keep_ref[:, cols] = acc[at, pl.ds(keep_at, part)]
            send_ref[:, cols] = acc[at, pl.ds(send_at, part)].astype(bf16)
        total = jnp.sum(tot[at, :], axis=1, keepdims=True)
        inner = jnp.sum(acc[at, :] * unit[at, :].astype(f32), axis=1, keepdims=True)
        extras.append((total, inner, cos_row[at, :1]))
    extra = pack_extra(extras)
    keep_ref[:, width:] = extra
    send_ref[:, 2 * width :] = extra.astype(bf16)


def pack_extra(halves):
    shape = (halves[0][0].shape[0], lanes)
    lane = lax.broadcasted_iota(jnp.int32, shape, 1)
    out = jnp.zeros(shape, f32)
    k = 0
    for values in halves:
        for value in values:
            for piece in split3(value):
                out = jnp.where(lane == k, piece, out)
                k += 1
    return out


def unpack_extra(extra):
    halves = []
    for h in range(2):
        values = []
        for k in range(3 * h, 3 * h + 3):
            values.append(
                extra[:, 3 * k : 3 * k + 1]
                + extra[:, 3 * k + 1 : 3 * k + 2]
                + extra[:, 3 * k + 2 : 3 * k + 3]
            )
        halves.append(values)
    return halves


def class_pass(where, gathered, centres):
    rows = gathered.shape[0]
    images = 2 * rows
    count, width = centres.shape
    return pl.pallas_call(
        class_kernel,
        in_specs=[
            pl.BlockSpec(memory_space=pltpu.SMEM),
            pl.BlockSpec(memory_space=pltpu.VMEM),
            pl.BlockSpec(memory_space=pltpu.HBM),
        ],
        out_shape=(
            jax.ShapeDtypeStruct((rows, width + lanes), f32),
            jax.ShapeDtypeStruct((rows, width), bf16),
            jax.ShapeDtypeStruct((rows, 2 * width + lanes), bf16),
        ),
        scratch_shapes=[
            pltpu.VMEM((count, width), bf16),
            pltpu.VMEM((images, width), bf16),
            pltpu.VMEM((images, width), f32),
            pltpu.VMEM((images, lanes), f32),
            pltpu.VMEM((images, lanes), f32),
            pltpu.VMEM((8, images + lanes), jnp.int32),
            pltpu.SMEM((8, images + lanes), jnp.int32),
            pltpu.SMEM((images + 1,), jnp.int32),
            pltpu.SemaphoreType.DMA,
            pltpu.SemaphoreType.DMA((pieces,)),
        ],
        compiler_params=params(48),
        cost_estimate=pl.CostEstimate(
            flops=4 * images * count * width,
            bytes_accessed=2 * count * width,
            transcendentals=images * count,
        ),
        name="class_pass",
    )(where, gathered, centres)


def pair_kernel(keep_ref, keep_row_ref, got_ref, out_ref):
    rows, width = keep_row_ref.shape
    half, part = width // 2, width // 4
    summed = keep_ref[...] + jnp.concatenate(
        [got_ref[:, :width].astype(f32), got_ref[:, 2 * width :].astype(f32)], axis=1
    )
    target = keep_row_ref[...] + got_ref[:, width : 2 * width]
    extra = pack_extra(unpack_extra(summed[:, width:])).astype(bf16)
    for group in range(2):
        at = slice(group * rows, (group + 1) * rows)
        for h in range(2):
            cols = slice(h * half + group * part, h * half + (group + 1) * part)
            out_ref[at, h * part : (h + 1) * part] = summed[:, cols].astype(bf16)
            out_ref[at, half + h * part : half + (h + 1) * part] = target[:, cols]
        out_ref[at, width:] = extra


def pair_sum(keep, keep_rows, got):
    rows, width = keep_rows.shape
    return pl.pallas_call(
        pair_kernel,
        out_shape=pltpu.VMEM((2 * rows, width + lanes), bf16),
        compiler_params=params(12),
        name="pair_sum",
    )(keep, keep_rows, got)


def home_kernel(where_ref, got_ref, unit_ref, len_ref, loss_ref, grad_ref):
    column = where_ref[2]
    images, part = grad_ref.shape
    half = images // 2
    summed = jnp.zeros((images, got_ref.shape[1]), f32)
    for k in range(0, got_ref.shape[0], images):
        summed = summed + got_ref[k : k + images, :].astype(f32)
    summed = summed[:half] + summed[half:]
    row = lax.broadcasted_iota(jnp.int32, (half, images), 0)
    lane = lax.broadcasted_iota(jnp.int32, (half, images), 1)
    loss_row = jnp.zeros((1, images), f32)
    for h, (rest, inner, cos) in enumerate(unpack_extra(summed[:, 4 * part :])):
        at = slice(h * half, (h + 1) * half)
        gradient = summed[:, h * part : (h + 1) * part]
        target = summed[:, (2 + h) * part : (3 + h) * part]
        shifted, slope = arc_target(cos)
        own = jnp.exp(logit_scale * shifted)
        total = rest + own
        loss = jnp.log(total) - logit_scale * shifted
        loss_row += jnp.sum(jnp.where(lane == row + h * half, loss, 0.0), axis=0, keepdims=True)
        weight = (logit_scale * ((own / total - 1.0) * slope)).astype(bf16).astype(f32)
        scale = logit_scale / total
        dots = inner * scale + weight * cos
        unit = unit_ref[at, pl.ds(pl.multiple_of(column * part, part), part)]
        grad_ref[at, :] = (gradient * scale + weight * target - unit * dots) / len_ref[at, :1]
    loss_ref[...] = loss_row


def home(where, got, unit, length):
    images = unit.shape[0]
    part = unit.shape[1] // 4
    return pl.pallas_call(
        home_kernel,
        in_specs=[
            pl.BlockSpec(memory_space=pltpu.SMEM),
            pl.BlockSpec(memory_space=pltpu.VMEM),
            pl.BlockSpec(memory_space=pltpu.VMEM),
            pl.BlockSpec(memory_space=pltpu.VMEM),
        ],
        out_shape=(
            jax.ShapeDtypeStruct((1, images), f32),
            jax.ShapeDtypeStruct((images, part), f32),
        ),
        compiler_params=params(12),
        name="home",
    )(where, got, unit, length)


swap = [(0, 1), (1, 0)]


def shards(tokens, norm_gain, weight_in, weight_out, final_gain, centres, labels):
    images, tok_count, width = tokens.shape
    count = centres.shape[0]
    homes = lax.axis_size("dp")
    core = lax.axis_index("core")
    column = lax.axis_index("z_hi") * 2 + core
    offset = (column * homes + lax.axis_index("dp")) * count
    where = jnp.stack([offset, core, column]).astype(jnp.int32)

    partial = feed_forward(
        tokens.reshape(-1, width), norm_gain[None], weight_in, weight_out
    )
    partial = partial + lax.ppermute(partial, "core", swap)
    other = lax.ppermute(partial, "z_hi", swap)
    send, unit, length = unit_rows_of(where, labels, partial, other, final_gain[None], homes)
    gathered = lax.all_to_all(send, "dp", 0, 0, tiled=True)
    keep, keep_rows, give = class_pass(where, gathered, centres)
    got = lax.ppermute(give, "core", swap)
    paired = pair_sum(keep, keep_rows, got)
    arrived = lax.all_to_all(paired, ("z_hi", "dp"), 0, 0, tiled=True)
    loss, grad = home(where, arrived, unit, length)
    return (loss[0], grad)


def solution(mesh):
    fine = Mesh(mesh.devices.reshape(2, 2, -1), ("z_hi", "core", "dp"))
    mp = ("z_hi", "core")
    return jax.shard_map(
        shards,
        mesh=fine,
        in_specs=(
            P("dp", None, None),
            P(),
            P(None, mp),
            P(mp, None),
            P(),
            P((*mp, "dp"), None),
            P("dp"),
        ),
        out_specs=(P("dp"), P("dp", mp)),
        check_vma=False,
    )
```

```python
import functools
import math

import jax
import jax.numpy as jnp
from jax import lax
from jax.experimental import pallas as pl
from jax.experimental.pallas import tpu as pltpu
from jax.sharding import Mesh, PartitionSpec as P

logit_scale = 64.0
angle_margin = 0.5
exp2_scale = logit_scale / math.log(2.0)
lanes = 128
digits = 3
pieces = 8
columns = 256
batch = 4
f32 = jnp.float32
bf16 = jnp.bfloat16


def params(mebibytes):
    return pltpu.CompilerParams(vmem_limit_bytes=mebibytes * 1024 * 1024)


def arc_target(target_cos):
    target_sine = jnp.sqrt(jnp.maximum(1.0 - target_cos * target_cos, 0.01))
    inside = target_cos > -math.cos(angle_margin)
    shifted = jnp.where(
        inside,
        target_cos * math.cos(angle_margin) - target_sine * math.sin(angle_margin),
        target_cos - angle_margin * math.sin(angle_margin),
    )
    margin_slope = jnp.where(
        inside, math.cos(angle_margin) + math.sin(angle_margin) * target_cos / target_sine, 1.0
    )
    return (shifted, margin_slope)


def layer_norm(values, gain_vec):
    average = jnp.mean(values, axis=-1, keepdims=True)
    centred = values - average
    variance = jnp.mean(centred * centred, axis=-1, keepdims=True)
    return centred * lax.rsqrt(variance + 1e-06) * gain_vec


def split3(value):
    hi = value.astype(bf16).astype(f32)
    mid = (value - hi).astype(bf16).astype(f32)
    return hi, mid, value - hi - mid


toks = 64


def ffn_kernel(tokens_ref, gain_ref, win_ref, wout_hbm, out_ref, mean_ref, tok_ref, wout, sem):
    step = pl.program_id(0)
    block, width = tokens_ref.shape
    sub = 256
    per = sub // toks
    fetch = pltpu.make_async_copy(wout_hbm, wout, sem)

    @pl.when(step == 0)
    def _():
        fetch.start()

    image = lax.broadcasted_iota(jnp.int32, (8, sub), 0)
    member = (lax.broadcasted_iota(jnp.int32, (8, sub), 1) // toks == image).astype(f32).astype(bf16)
    for k in range(block // sub):
        rows = tokens_ref[k * sub : (k + 1) * sub, :]
        normed = layer_norm(rows.astype(f32), gain_ref[...]).astype(bf16)
        pre = jnp.dot(normed, win_ref[...], preferred_element_type=f32)
        hidden = (0.5 * pre * (1.0 + lax.erf(pre * math.sqrt(0.5)))).astype(bf16)
        mean = jnp.dot(member, hidden, preferred_element_type=f32) * (1.0 / toks)
        tok = jnp.dot(member, rows, preferred_element_type=f32) * (0.25 / toks)
        for q in range(per):
            at = pl.ds(step * (block // toks) + k * per + q, 1)
            mean_ref[at, :] = mean[q : q + 1]
            tok_ref[at, :] = tok[q : q + 1]

    @pl.when(step == pl.num_programs(0) - 1)
    def _():
        fetch.wait()
        mean = mean_ref[...]
        hi = mean.astype(bf16)
        lo = (mean - hi.astype(f32)).astype(bf16)
        both = jnp.dot(jnp.concatenate([hi, lo], axis=0), wout[...], preferred_element_type=f32)
        images = mean.shape[0]
        out_ref[...] = both[:images] + both[images:] + tok_ref[...]


def feed_forward(tokens, gain, weight_in, weight_out):
    rows, width = tokens.shape
    hidden = weight_in.shape[1]
    images = rows // toks
    block = 512
    return pl.pallas_call(
        ffn_kernel,
        grid=(rows // block,),
        in_specs=[
            pl.BlockSpec((block, width), lambda i: (i, 0)),
            pl.BlockSpec((1, width), lambda i: (0, 0)),
            pl.BlockSpec((width, hidden), lambda i: (0, 0)),
            pl.BlockSpec(memory_space=pltpu.HBM),
        ],
        out_specs=pl.BlockSpec((images, width), lambda i: (0, 0)),
        out_shape=pltpu.VMEM((images, width), f32),
        scratch_shapes=[
            pltpu.VMEM((images, hidden), f32),
            pltpu.VMEM((images, width), f32),
            pltpu.VMEM((hidden, width), bf16),
            pltpu.SemaphoreType.DMA,
        ],
        compiler_params=params(58),
        cost_estimate=pl.CostEstimate(
            flops=2 * rows * width * hidden, bytes_accessed=6 << 20, transcendentals=rows * hidden
        ),
        name="ffn",
    )(tokens, gain, weight_in, weight_out)


def unit_kernel(where_ref, labels_ref, mine_ref, other_ref, gain_ref, send_ref, unit_ref, len_ref):
    images, width = mine_ref.shape
    pooled = mine_ref[...] + other_ref[...]
    embedding = layer_norm(pooled, gain_ref[...])
    length = jnp.sqrt(jnp.sum(embedding * embedding, axis=1, keepdims=True) + 1e-06)
    unit = (embedding / length).astype(bf16).astype(f32)
    half = images // 2
    first = where_ref[1] == 1
    row = lax.broadcasted_iota(jnp.int32, (half, lanes), 0)
    lane = lax.broadcasted_iota(jnp.int32, (half, lanes), 1)
    label = jnp.zeros((half, lanes), jnp.int32)
    for r in range(half):
        label = jnp.where(
            row == r, jnp.where(first, labels_ref[r], labels_ref[half + r]), label
        )
    coded = jnp.where(
        lane == 0,
        label & 127,
        jnp.where(lane == 1, (label >> 7) & 127, jnp.where(lane == 2, label >> 14, 0)),
    )
    chosen = jnp.where(first, unit[:half], unit[half:])
    payload = jnp.concatenate([chosen, coded.astype(f32)], axis=1)
    payload = jnp.concatenate([payload, payload], axis=0).astype(bf16)
    for d in range(send_ref.shape[0] // images):
        send_ref[d * images : (d + 1) * images, :] = payload
    unit_ref[...] = unit
    len_ref[...] = jnp.broadcast_to(length, (images, lanes))


def unit_rows_of(where, labels, mine, other, gain, homes):
    images, width = mine.shape
    return pl.pallas_call(
        unit_kernel,
        in_specs=[
            pl.BlockSpec(memory_space=pltpu.SMEM),
            pl.BlockSpec(memory_space=pltpu.SMEM),
            pl.BlockSpec(memory_space=pltpu.VMEM),
            pl.BlockSpec(memory_space=pltpu.VMEM),
            pl.BlockSpec(memory_space=pltpu.VMEM),
        ],
        out_shape=(
            pltpu.VMEM((homes * images // 2, width + lanes), bf16),
            jax.ShapeDtypeStruct((images, width), f32),
            jax.ShapeDtypeStruct((images, lanes), f32),
        ),
        compiler_params=params(8),
        name="unit_rows",
    )(where, labels, mine, other, gain)


def digit_weights(shape, axis):
    at = lax.broadcasted_iota(jnp.int32, shape, axis)
    return jnp.where(
        at == 0, 1.0, jnp.where(at == 1, 128.0, jnp.where(at == 2, 16384.0, 0.0))
    ).astype(bf16)


group_size = 16


def class_kernel(second, where_ref, all_ref, centres_ref, *refs):
    if second:
        inverse_ref, keep_ref, keep_row_ref, send_ref, *refs = refs
    else:
        keep_ref, keep_row_ref, send_ref, inverse_ref, *refs = refs
    held, acc, tot, cos_row, lab, lab_s, found_s, lab_sem, sems = refs
    offset, core = where_ref[0], where_ref[1]
    images = all_ref.shape[0]
    count, width = centres_ref.shape
    piece = count // pieces
    half, part = width // 2, width // 4
    groups = images // group_size

    def fetch(i):
        at = pl.ds(pl.multiple_of(i * piece, piece), piece)
        return pltpu.make_async_copy(centres_ref.at[at, :], held.at[at, :], sems.at[i])

    for i in range(3):
        fetch(i).start()

    coded = all_ref[:, width:]
    turned = (((1,), (1,)), ((), ()))
    row = lax.dot_general(
        digit_weights((8, lanes), 1), coded, turned, preferred_element_type=f32
    ).astype(jnp.int32) - offset
    member = lax.broadcasted_iota(jnp.int32, (images, lanes), 0) // group_size
    member = (member == lax.broadcasted_iota(jnp.int32, (images, lanes), 1)).astype(bf16)
    inside = jnp.logical_and(row >= 0, row < count).astype(f32).astype(bf16)
    lab[:, :images] = row
    lab[:, images:] = jnp.dot(inside, member, preferred_element_type=f32).astype(jnp.int32)
    copy = pltpu.make_async_copy(lab, lab_s, lab_sem)
    copy.start()
    local = (
        jnp.dot(coded, digit_weights((lanes, lanes), 0), preferred_element_type=f32)
    ).astype(jnp.int32) - offset
    acc[...] = jnp.zeros(acc.shape, f32)
    tot[...] = jnp.zeros(tot.shape, f32)
    cos_row[...] = jnp.zeros(cos_row.shape, f32)
    keep_row_ref[...] = jnp.zeros(keep_row_ref.shape, bf16)
    send_ref[:, half:width] = jnp.zeros((images, half), bf16)
    copy.wait()
    found_s[images] = 0

    def look(g, c):
        @pl.when(lab_s[0, images + g] > 0)
        def _():
            for k in range(group_size):
                i = g * group_size + k
                at = lab_s[0, i]

                @pl.when(jnp.logical_and(at >= 0, at < count))
                def _():
                    n = found_s[images]
                    found_s[n] = i
                    found_s[images] = n + 1

        return c

    lax.fori_loop(0, groups, look, 0)

    diagonal = lax.broadcasted_iota(jnp.int32, (lanes, lanes), 0) == lax.broadcasted_iota(
        jnp.int32, (lanes, lanes), 1
    )

    def step(first, joined, ahead):
        base = pl.multiple_of(first * piece, piece)
        block = joined * piece
        for q in range(joined):
            fetch(first + q).wait()
        for q in ahead:
            fetch(first + q).start()

        centres = held[pl.ds(base, block), :]
        cosine = lax.dot_general(
            all_ref[:, :width], centres, turned, preferred_element_type=f32
        )
        lane = lax.broadcasted_iota(jnp.int32, (images, lanes), 1) + base
        parts = []
        total = tot[...]
        for j in range(block // lanes):
            at = pl.ds(base + j * lanes, lanes)
            if second:
                inverse = inverse_ref[:, at]
            else:
                wide = held[at, :].astype(f32)
                square = jnp.sum(wide * wide, axis=1, keepdims=True)
                square = jnp.sum(jnp.where(diagonal, square, 0.0), axis=0, keepdims=True)
                inverse = lax.rsqrt(square + 1e-06)
                inverse_ref[:, at] = inverse
            value = jnp.exp2(cosine[:, j * lanes : (j + 1) * lanes] * (inverse * exp2_scale))
            value = jnp.where(local == lane + j * lanes, 0.0, value)
            total = total + value
            parts.append((value * inverse).astype(bf16))
        tot[...] = total
        weight = jnp.concatenate(parts, axis=1)
        for n in range(0, width, columns):
            cols = slice(n, n + columns)
            acc[:, cols] += jnp.dot(weight, centres[:, cols], preferred_element_type=f32)

    def pair(t, c):
        step(1 + 2 * t, 2, (4, 5))
        return c

    step(0, 1, (3, 4))
    lax.fori_loop(0, (pieces - 6) // 2, pair, 0)
    step(pieces - 5, 2, (4,))
    step(pieces - 3, 2, ())
    step(pieces - 1, 1, ())

    sub = lax.broadcasted_iota(jnp.int32, (16, width), 0)

    def take(k, c):
        ready = []
        for q in range(batch):
            i = found_s[jnp.minimum(k * batch + q, found_s[images] - 1)]
            at = lab_s[0, i]
            raw = held[pl.ds(pl.multiple_of((at >> 4) << 4, 16), 16), :].astype(f32)
            raw = jnp.sum(jnp.where(sub == (at & 15), raw, 0.0), axis=0, keepdims=True)
            found = raw * lax.rsqrt(jnp.sum(raw * raw, axis=1, keepdims=True) + 1e-06)
            found = found.astype(bf16).astype(f32)
            mine = sub == (i & 15)
            here = pl.ds(pl.multiple_of((i >> 4) << 4, 16), 16)
            image = all_ref[here, :width].astype(f32)
            cos = jnp.sum(jnp.where(mine, image * found, 0.0), axis=1, keepdims=True)
            even = jnp.concatenate([found[:, :part], found[:, half : half + part]], axis=1)
            odd = jnp.concatenate([found[:, part:half], found[:, half + part :]], axis=1)
            kept = jnp.where(core == 0, even, odd)
            sent = jnp.where(core == 0, odd, even)
            ready.append((mine, here, cos, kept, sent))
        for mine, here, cos, kept, sent in ready:
            cos_row[here, :] = jnp.where(mine[:, :lanes], cos, cos_row[here, :])
            for ref, start, value in ((keep_row_ref, 0, kept), (send_ref, half, sent)):
                cols = slice(start, start + half)
                ref[here, cols] = jnp.where(
                    mine[:, :half], value, ref[here, cols].astype(f32)
                ).astype(bf16)
        return c

    lax.fori_loop(0, (found_s[images] + batch - 1) // batch, take, 0)

    for group in range(2):
        cols = slice(group * part, (group + 1) * part)
        keep_at = pl.multiple_of((2 * group + core) * part, part)
        send_at = pl.multiple_of((2 * group + 1 - core) * part, part)
        keep_ref[:, cols] = acc[:, pl.ds(keep_at, part)]
        send_ref[:, cols] = acc[:, pl.ds(send_at, part)].astype(bf16)
    total = jnp.sum(tot[...], axis=1, keepdims=True)
    inner = jnp.sum(acc[...] * all_ref[:, :width].astype(f32), axis=1, keepdims=True)
    extra = pack_extra([(total, inner, cos_row[:, :1])])
    keep_ref[:, half:] = extra
    send_ref[:, width:] = extra.astype(bf16)


def pack_extra(halves):
    shape = (halves[0][0].shape[0], lanes)
    lane = lax.broadcasted_iota(jnp.int32, shape, 1)
    out = jnp.zeros(shape, f32)
    k = 0
    for values in halves:
        for value in values:
            for piece in split3(value):
                out = jnp.where(lane == k, piece, out)
                k += 1
    return out


def unpack_extra(extra, halves_held):
    halves = []
    for h in range(halves_held):
        values = []
        for k in range(3 * h, 3 * h + 3):
            values.append(
                extra[:, 3 * k : 3 * k + 1]
                + extra[:, 3 * k + 1 : 3 * k + 2]
                + extra[:, 3 * k + 2 : 3 * k + 3]
            )
        halves.append(values)
    return halves


def class_pass(where, gathered, centres, inverse=None):
    images = gathered.shape[0]
    count, width = centres.shape
    half = width // 2
    second = inverse is not None
    vmem = pl.BlockSpec(memory_space=pltpu.VMEM)
    outs = (
        jax.ShapeDtypeStruct((images, half + lanes), f32),
        jax.ShapeDtypeStruct((images, half), bf16),
        jax.ShapeDtypeStruct((images, width + lanes), bf16),
    )
    return pl.pallas_call(
        functools.partial(class_kernel, second),
        in_specs=[
            pl.BlockSpec(memory_space=pltpu.SMEM),
            vmem,
            pl.BlockSpec(memory_space=pltpu.HBM),
        ]
        + [vmem] * second,
        out_shape=outs if second else (*outs, jax.ShapeDtypeStruct((1, count), f32)),
        scratch_shapes=[
            pltpu.VMEM((count, width), bf16),
            pltpu.VMEM((images, width), f32),
            pltpu.VMEM((images, lanes), f32),
            pltpu.VMEM((images, lanes), f32),
            pltpu.VMEM((8, images + lanes), jnp.int32),
            pltpu.SMEM((8, images + lanes), jnp.int32),
            pltpu.SMEM((images + 1,), jnp.int32),
            pltpu.SemaphoreType.DMA,
            pltpu.SemaphoreType.DMA((pieces,)),
        ],
        compiler_params=params(48),
        cost_estimate=pl.CostEstimate(
            flops=4 * images * count * width,
            bytes_accessed=2 * count * width,
            transcendentals=images * count,
        ),
        name="class_pass",
    )(where, gathered, centres, *([inverse] if second else []))


def pair_kernel(where_ref, *refs):
    out_ref = refs[-1]
    rows, half = refs[1].shape
    width, part = 2 * half, half // 2
    sums, targets, extras = [], [], []
    for keep_ref, keep_row_ref, got_ref in (refs[0:3], refs[3:6]):
        sums.append((keep_ref[:, :half] + got_ref[:, :half].astype(f32)).astype(bf16))
        targets.append(keep_row_ref[...] + got_ref[:, half:width])
        extras.append(keep_ref[:, half:] + got_ref[:, width:].astype(f32))
    swapped = where_ref[1] == 0
    extra = pack_extra(
        [
            unpack_extra(jnp.where(swapped, extras[1 - h], extras[h]), 1)[0]
            for h in range(2)
        ]
    ).astype(bf16)
    for h in range(2):
        summed = jnp.where(swapped, sums[1 - h], sums[h])
        target = jnp.where(swapped, targets[1 - h], targets[h])
        for group in range(2):
            at = slice(group * rows, (group + 1) * rows)
            cols = slice(group * part, (group + 1) * part)
            out_ref[at, h * part : (h + 1) * part] = summed[:, cols]
            out_ref[at, half + h * part : half + (h + 1) * part] = target[:, cols]
    for group in range(2):
        out_ref[group * rows : (group + 1) * rows, width:] = extra


def pair_sum(where, *arrays):
    rows, half = arrays[1].shape
    return pl.pallas_call(
        pair_kernel,
        in_specs=[pl.BlockSpec(memory_space=pltpu.SMEM)]
        + [pl.BlockSpec(memory_space=pltpu.VMEM)] * len(arrays),
        out_shape=pltpu.VMEM((2 * rows, 2 * half + lanes), bf16),
        compiler_params=params(12),
        name="pair_sum",
    )(where, *arrays)


def home_kernel(where_ref, got_ref, unit_ref, len_ref, loss_ref, grad_ref):
    column = where_ref[2]
    images, part = grad_ref.shape
    half = images // 2
    summed = jnp.zeros((images, got_ref.shape[1]), f32)
    for k in range(0, got_ref.shape[0], images):
        summed = summed + got_ref[k : k + images, :].astype(f32)
    summed = summed[:half] + summed[half:]
    row = lax.broadcasted_iota(jnp.int32, (half, images), 0)
    lane = lax.broadcasted_iota(jnp.int32, (half, images), 1)
    loss_row = jnp.zeros((1, images), f32)
    for h, (rest, inner, cos) in enumerate(unpack_extra(summed[:, 4 * part :], 2)):
        at = slice(h * half, (h + 1) * half)
        gradient = summed[:, h * part : (h + 1) * part]
        target = summed[:, (2 + h) * part : (3 + h) * part]
        shifted, slope = arc_target(cos)
        own = jnp.exp(logit_scale * shifted)
        total = rest + own
        loss = jnp.log(total) - logit_scale * shifted
        loss_row += jnp.sum(jnp.where(lane == row + h * half, loss, 0.0), axis=0, keepdims=True)
        weight = (logit_scale * ((own / total - 1.0) * slope)).astype(bf16).astype(f32)
        scale = logit_scale / total
        dots = inner * scale + weight * cos
        unit = unit_ref[at, pl.ds(pl.multiple_of(column * part, part), part)]
        grad_ref[at, :] = (gradient * scale + weight * target - unit * dots) / len_ref[at, :1]
    loss_ref[...] = loss_row


def home(where, got, unit, length):
    images = unit.shape[0]
    part = unit.shape[1] // 4
    return pl.pallas_call(
        home_kernel,
        in_specs=[
            pl.BlockSpec(memory_space=pltpu.SMEM),
            pl.BlockSpec(memory_space=pltpu.VMEM),
            pl.BlockSpec(memory_space=pltpu.VMEM),
            pl.BlockSpec(memory_space=pltpu.VMEM),
        ],
        out_shape=(
            jax.ShapeDtypeStruct((1, images), f32),
            jax.ShapeDtypeStruct((images, part), f32),
        ),
        compiler_params=params(12),
        name="home",
    )(where, got, unit, length)


swap = [(0, 1), (1, 0)]


def shards(tokens, norm_gain, weight_in, weight_out, final_gain, centres, labels):
    images, tok_count, width = tokens.shape
    count = centres.shape[0]
    homes = lax.axis_size("dp")
    core = lax.axis_index("core")
    column = lax.axis_index("z_hi") * 2 + core
    offset = (column * homes + lax.axis_index("dp")) * count
    where = jnp.stack([offset, core, column]).astype(jnp.int32)

    partial = feed_forward(
        tokens.reshape(-1, width), norm_gain[None], weight_in, weight_out
    )
    partial = partial + lax.ppermute(partial, "core", swap)
    other = lax.ppermute(partial, "z_hi", swap)
    send, unit, length = unit_rows_of(where, labels, partial, other, final_gain[None], homes)
    gathered = lax.all_to_all(send, "dp", 0, 0, tiled=True)
    crossed = lax.ppermute(gathered, "core", swap)
    keep, keep_rows, give, inverse = class_pass(where, gathered, centres)
    got = lax.ppermute(give, "core", swap)
    keep_2, keep_rows_2, give_2 = class_pass(where, crossed, centres, inverse)
    got_2 = lax.ppermute(give_2, "core", swap)
    paired = pair_sum(where, keep, keep_rows, got_2, keep_2, keep_rows_2, got)
    arrived = lax.all_to_all(paired, ("z_hi", "dp"), 0, 0, tiled=True)
    loss, grad = home(where, arrived, unit, length)
    return (loss[0], grad)


def solution(mesh):
    fine = Mesh(mesh.devices.reshape(2, 2, -1), ("z_hi", "core", "dp"))
    mp = ("z_hi", "core")
    return jax.shard_map(
        shards,
        mesh=fine,
        in_specs=(
            P("dp", None, None),
            P(),
            P(None, mp),
            P(mp, None),
            P(),
            P((*mp, "dp"), None),
            P("dp"),
        ),
        out_specs=(P("dp"), P("dp", mp)),
        check_vma=False,
    )
```

```python
import functools
import math

import jax
import jax.numpy as jnp
from jax import lax
from jax.experimental import pallas as pl
from jax.experimental.pallas import tpu as pltpu
from jax.sharding import Mesh, PartitionSpec as P

logit_scale = 64.0
angle_margin = 0.5
exp2_scale = logit_scale / math.log(2.0)
lanes = 128
digits = 3
pieces = 8
columns = 256
batch = 4
f32 = jnp.float32
bf16 = jnp.bfloat16


def params(mebibytes):
    return pltpu.CompilerParams(vmem_limit_bytes=mebibytes * 1024 * 1024)


def arc_target(target_cos):
    target_sine = jnp.sqrt(jnp.maximum(1.0 - target_cos * target_cos, 0.01))
    inside = target_cos > -math.cos(angle_margin)
    shifted = jnp.where(
        inside,
        target_cos * math.cos(angle_margin) - target_sine * math.sin(angle_margin),
        target_cos - angle_margin * math.sin(angle_margin),
    )
    margin_slope = jnp.where(
        inside, math.cos(angle_margin) + math.sin(angle_margin) * target_cos / target_sine, 1.0
    )
    return (shifted, margin_slope)


def layer_norm(values, gain_vec):
    average = jnp.mean(values, axis=-1, keepdims=True)
    centred = values - average
    variance = jnp.mean(centred * centred, axis=-1, keepdims=True)
    return centred * lax.rsqrt(variance + 1e-06) * gain_vec


def split3(value):
    hi = value.astype(bf16).astype(f32)
    mid = (value - hi).astype(bf16).astype(f32)
    return hi, mid, value - hi - mid


toks = 64


def ffn_kernel(tokens_ref, gain_ref, win_ref, wout_hbm, out_ref, mean_ref, tok_ref, wout, sem):
    step = pl.program_id(0)
    block, width = tokens_ref.shape
    sub = 256
    per = sub // toks
    fetch = pltpu.make_async_copy(wout_hbm, wout, sem)

    @pl.when(step == 0)
    def _():
        fetch.start()

    image = lax.broadcasted_iota(jnp.int32, (8, sub), 0)
    member = (lax.broadcasted_iota(jnp.int32, (8, sub), 1) // toks == image).astype(f32).astype(bf16)
    for k in range(block // sub):
        rows = tokens_ref[k * sub : (k + 1) * sub, :]
        normed = layer_norm(rows.astype(f32), gain_ref[...]).astype(bf16)
        pre = jnp.dot(normed, win_ref[...], preferred_element_type=f32)
        hidden = (0.5 * pre * (1.0 + lax.erf(pre * math.sqrt(0.5)))).astype(bf16)
        mean = jnp.dot(member, hidden, preferred_element_type=f32) * (1.0 / toks)
        tok = jnp.dot(member, rows, preferred_element_type=f32) * (0.25 / toks)
        for q in range(per):
            at = pl.ds(step * (block // toks) + k * per + q, 1)
            mean_ref[at, :] = mean[q : q + 1]
            tok_ref[at, :] = tok[q : q + 1]

    @pl.when(step == pl.num_programs(0) - 1)
    def _():
        fetch.wait()
        mean = mean_ref[...]
        hi = mean.astype(bf16)
        lo = (mean - hi.astype(f32)).astype(bf16)
        both = jnp.dot(jnp.concatenate([hi, lo], axis=0), wout[...], preferred_element_type=f32)
        images = mean.shape[0]
        out_ref[...] = both[:images] + both[images:] + tok_ref[...]


def feed_forward(tokens, gain, weight_in, weight_out):
    rows, width = tokens.shape
    hidden = weight_in.shape[1]
    images = rows // toks
    block = 512
    return pl.pallas_call(
        ffn_kernel,
        grid=(rows // block,),
        in_specs=[
            pl.BlockSpec((block, width), lambda i: (i, 0)),
            pl.BlockSpec((1, width), lambda i: (0, 0)),
            pl.BlockSpec((width, hidden), lambda i: (0, 0)),
            pl.BlockSpec(memory_space=pltpu.HBM),
        ],
        out_specs=pl.BlockSpec((images, width), lambda i: (0, 0)),
        out_shape=pltpu.VMEM((images, width), f32),
        scratch_shapes=[
            pltpu.VMEM((images, hidden), f32),
            pltpu.VMEM((images, width), f32),
            pltpu.VMEM((hidden, width), bf16),
            pltpu.SemaphoreType.DMA,
        ],
        compiler_params=params(58),
        cost_estimate=pl.CostEstimate(
            flops=2 * rows * width * hidden, bytes_accessed=6 << 20, transcendentals=rows * hidden
        ),
        name="ffn",
    )(tokens, gain, weight_in, weight_out)


def unit_kernel(where_ref, labels_ref, mine_ref, other_ref, gain_ref, send_ref, unit_ref, len_ref):
    images, width = mine_ref.shape
    pooled = mine_ref[...] + other_ref[...]
    embedding = layer_norm(pooled, gain_ref[...])
    length = jnp.sqrt(jnp.sum(embedding * embedding, axis=1, keepdims=True) + 1e-06)
    unit = (embedding / length).astype(bf16).astype(f32)
    half = images // 2
    first = where_ref[1] == 1
    row = lax.broadcasted_iota(jnp.int32, (half, lanes), 0)
    lane = lax.broadcasted_iota(jnp.int32, (half, lanes), 1)
    label = jnp.zeros((half, lanes), jnp.int32)
    for r in range(half):
        label = jnp.where(
            row == r, jnp.where(first, labels_ref[r], labels_ref[half + r]), label
        )
    coded = jnp.where(
        lane == 0,
        label & 127,
        jnp.where(lane == 1, (label >> 7) & 127, jnp.where(lane == 2, label >> 14, 0)),
    )
    chosen = jnp.where(first, unit[:half], unit[half:])
    payload = jnp.concatenate([chosen, coded.astype(f32)], axis=1)
    payload = jnp.concatenate([payload, payload], axis=0).astype(bf16)
    for d in range(send_ref.shape[0] // images):
        send_ref[d * images : (d + 1) * images, :] = payload
    unit_ref[...] = unit
    len_ref[...] = jnp.broadcast_to(length, (images, lanes))


def unit_rows_of(where, labels, mine, other, gain, homes):
    images, width = mine.shape
    return pl.pallas_call(
        unit_kernel,
        in_specs=[
            pl.BlockSpec(memory_space=pltpu.SMEM),
            pl.BlockSpec(memory_space=pltpu.SMEM),
            pl.BlockSpec(memory_space=pltpu.VMEM),
            pl.BlockSpec(memory_space=pltpu.VMEM),
            pl.BlockSpec(memory_space=pltpu.VMEM),
        ],
        out_shape=(
            pltpu.VMEM((homes * images // 2, width + lanes), bf16),
            jax.ShapeDtypeStruct((images, width), f32),
            jax.ShapeDtypeStruct((images, lanes), f32),
        ),
        compiler_params=params(8),
        name="unit_rows",
    )(where, labels, mine, other, gain)


def digit_weights(shape, axis):
    at = lax.broadcasted_iota(jnp.int32, shape, axis)
    return jnp.where(
        at == 0, 1.0, jnp.where(at == 1, 128.0, jnp.where(at == 2, 16384.0, 0.0))
    ).astype(bf16)


group_size = 16


def class_kernel(second, where_ref, all_ref, centres_ref, *refs):
    if second:
        inverse_ref, keep_ref, keep_row_ref, send_ref, *refs = refs
    else:
        keep_ref, keep_row_ref, send_ref, inverse_ref, *refs = refs
    held, acc, tot, cos_row, lab, lab_s, found_s, lab_sem, sems = refs
    offset, core = where_ref[0], where_ref[1]
    images = all_ref.shape[0]
    count, width = centres_ref.shape
    piece = count // pieces
    half, part = width // 2, width // 4
    groups = images // group_size

    def fetch(i):
        at = pl.ds(pl.multiple_of(i * piece, piece), piece)
        return pltpu.make_async_copy(centres_ref.at[at, :], held.at[at, :], sems.at[i])

    for i in range(3):
        fetch(i).start()

    coded = all_ref[:, width:]
    turned = (((1,), (1,)), ((), ()))
    row = lax.dot_general(
        digit_weights((8, lanes), 1), coded, turned, preferred_element_type=f32
    ).astype(jnp.int32) - offset
    member = lax.broadcasted_iota(jnp.int32, (images, lanes), 0) // group_size
    member = (member == lax.broadcasted_iota(jnp.int32, (images, lanes), 1)).astype(bf16)
    inside = jnp.logical_and(row >= 0, row < count).astype(f32).astype(bf16)
    lab[:, :images] = row
    lab[:, images:] = jnp.dot(inside, member, preferred_element_type=f32).astype(jnp.int32)
    copy = pltpu.make_async_copy(lab, lab_s, lab_sem)
    copy.start()
    local = (
        jnp.dot(coded, digit_weights((lanes, lanes), 0), preferred_element_type=f32)
    ).astype(jnp.int32) - offset
    acc[...] = jnp.zeros(acc.shape, f32)
    tot[...] = jnp.zeros(tot.shape, f32)
    cos_row[...] = jnp.zeros(cos_row.shape, f32)
    keep_row_ref[...] = jnp.zeros(keep_row_ref.shape, bf16)
    send_ref[:, half:width] = jnp.zeros((images, half), bf16)
    copy.wait()
    found_s[images] = 0

    def look(g, c):
        @pl.when(lab_s[0, images + g] > 0)
        def _():
            for k in range(group_size):
                i = g * group_size + k
                at = lab_s[0, i]

                @pl.when(jnp.logical_and(at >= 0, at < count))
                def _():
                    n = found_s[images]
                    found_s[n] = i
                    found_s[images] = n + 1

        return c

    lax.fori_loop(0, groups, look, 0)

    diagonal = lax.broadcasted_iota(jnp.int32, (lanes, lanes), 0) == lax.broadcasted_iota(
        jnp.int32, (lanes, lanes), 1
    )

    def step(first, joined, ahead):
        base = pl.multiple_of(first * piece, piece)
        block = joined * piece
        for q in range(joined):
            fetch(first + q).wait()
        for q in ahead:
            fetch(first + q).start()

        centres = held[pl.ds(base, block), :]
        cosine = lax.dot_general(
            all_ref[:, :width], centres, turned, preferred_element_type=f32
        )
        lane = lax.broadcasted_iota(jnp.int32, (images, lanes), 1) + base
        parts = []
        total = tot[...]
        for j in range(block // lanes):
            at = pl.ds(base + j * lanes, lanes)
            if second:
                inverse = inverse_ref[:, at]
            else:
                wide = held[at, :].astype(f32)
                square = jnp.sum(wide * wide, axis=1, keepdims=True)
                square = jnp.sum(jnp.where(diagonal, square, 0.0), axis=0, keepdims=True)
                inverse = lax.rsqrt(square + 1e-06)
                inverse_ref[:, at] = inverse
            value = jnp.exp2(cosine[:, j * lanes : (j + 1) * lanes] * (inverse * exp2_scale))
            value = jnp.where(local == lane + j * lanes, 0.0, value)
            total = total + value
            parts.append((value * inverse).astype(bf16))
        tot[...] = total
        weight = jnp.concatenate(parts, axis=1)
        for n in range(0, width, columns):
            cols = slice(n, n + columns)
            acc[:, cols] += jnp.dot(weight, centres[:, cols], preferred_element_type=f32)

    def pair(t, c):
        step(1 + 2 * t, 2, (4, 5))
        return c

    step(0, 1, (3, 4))
    lax.fori_loop(0, (pieces - 6) // 2, pair, 0)
    step(pieces - 5, 2, (4,))
    step(pieces - 3, 2, ())
    step(pieces - 1, 1, ())

    sub = lax.broadcasted_iota(jnp.int32, (16, width), 0)

    def take(k, c):
        ready = []
        for q in range(batch):
            i = found_s[jnp.minimum(k * batch + q, found_s[images] - 1)]
            at = lab_s[0, i]
            raw = held[pl.ds(pl.multiple_of((at >> 4) << 4, 16), 16), :].astype(f32)
            raw = jnp.sum(jnp.where(sub == (at & 15), raw, 0.0), axis=0, keepdims=True)
            found = raw * lax.rsqrt(jnp.sum(raw * raw, axis=1, keepdims=True) + 1e-06)
            found = found.astype(bf16).astype(f32)
            mine = sub == (i & 15)
            here = pl.ds(pl.multiple_of((i >> 4) << 4, 16), 16)
            image = all_ref[here, :width].astype(f32)
            cos = jnp.sum(jnp.where(mine, image * found, 0.0), axis=1, keepdims=True)
            even = jnp.concatenate([found[:, :part], found[:, half : half + part]], axis=1)
            odd = jnp.concatenate([found[:, part:half], found[:, half + part :]], axis=1)
            kept = jnp.where(core == 0, even, odd)
            sent = jnp.where(core == 0, odd, even)
            ready.append((mine, here, cos, kept, sent))
        for mine, here, cos, kept, sent in ready:
            cos_row[here, :] = jnp.where(mine[:, :lanes], cos, cos_row[here, :])
            for ref, start, value in ((keep_row_ref, 0, kept), (send_ref, half, sent)):
                cols = slice(start, start + half)
                ref[here, cols] = jnp.where(
                    mine[:, :half], value, ref[here, cols].astype(f32)
                ).astype(bf16)
        return c

    lax.fori_loop(0, (found_s[images] + batch - 1) // batch, take, 0)

    for group in range(2):
        cols = slice(group * part, (group + 1) * part)
        keep_at = pl.multiple_of((2 * group + core) * part, part)
        send_at = pl.multiple_of((2 * group + 1 - core) * part, part)
        keep_ref[:, cols] = acc[:, pl.ds(keep_at, part)]
        send_ref[:, cols] = acc[:, pl.ds(send_at, part)].astype(bf16)
    total = jnp.sum(tot[...], axis=1, keepdims=True)
    inner = jnp.sum(acc[...] * all_ref[:, :width].astype(f32), axis=1, keepdims=True)
    extra = pack_extra([(total, inner, cos_row[:, :1])])
    keep_ref[:, half:] = extra
    send_ref[:, width:] = extra.astype(bf16)


def pack_extra(halves):
    shape = (halves[0][0].shape[0], lanes)
    lane = lax.broadcasted_iota(jnp.int32, shape, 1)
    out = jnp.zeros(shape, f32)
    k = 0
    for values in halves:
        for value in values:
            for piece in split3(value):
                out = jnp.where(lane == k, piece, out)
                k += 1
    return out


def unpack_extra(extra, halves_held):
    halves = []
    for h in range(halves_held):
        values = []
        for k in range(3 * h, 3 * h + 3):
            values.append(
                extra[:, 3 * k : 3 * k + 1]
                + extra[:, 3 * k + 1 : 3 * k + 2]
                + extra[:, 3 * k + 2 : 3 * k + 3]
            )
        halves.append(values)
    return halves


def class_pass(where, gathered, centres, inverse=None):
    images = gathered.shape[0]
    count, width = centres.shape
    half = width // 2
    second = inverse is not None
    vmem = pl.BlockSpec(memory_space=pltpu.VMEM)
    outs = (
        jax.ShapeDtypeStruct((images, half + lanes), f32),
        jax.ShapeDtypeStruct((images, half), bf16),
        jax.ShapeDtypeStruct((images, width + lanes), bf16),
    )
    return pl.pallas_call(
        functools.partial(class_kernel, second),
        in_specs=[
            pl.BlockSpec(memory_space=pltpu.SMEM),
            vmem,
            pl.BlockSpec(memory_space=pltpu.HBM),
        ]
        + [vmem] * second,
        out_shape=outs if second else (*outs, jax.ShapeDtypeStruct((1, count), f32)),
        scratch_shapes=[
            pltpu.VMEM((count, width), bf16),
            pltpu.VMEM((images, width), f32),
            pltpu.VMEM((images, lanes), f32),
            pltpu.VMEM((images, lanes), f32),
            pltpu.VMEM((8, images + lanes), jnp.int32),
            pltpu.SMEM((8, images + lanes), jnp.int32),
            pltpu.SMEM((images + 1,), jnp.int32),
            pltpu.SemaphoreType.DMA,
            pltpu.SemaphoreType.DMA((pieces,)),
        ],
        compiler_params=params(48),
        cost_estimate=pl.CostEstimate(
            flops=4 * images * count * width,
            bytes_accessed=2 * count * width,
            transcendentals=images * count,
        ),
        name="class_pass",
    )(where, gathered, centres, *([inverse] if second else []))


def pair_kernel(where_ref, *refs):
    out_ref = refs[-1]
    rows, half = refs[1].shape
    width, part = 2 * half, half // 2
    core = where_ref[1]
    extras = []
    for h, (keep_ref, keep_row_ref, got_ref) in ((1 - core, refs[0:3]), (core, refs[3:6])):
        summed = (keep_ref[:, :half] + got_ref[:, :half].astype(f32)).astype(bf16)
        target = keep_row_ref[...] + got_ref[:, half:width]
        extras.append(keep_ref[:, half:] + got_ref[:, width:].astype(f32))
        sum_at = pl.ds(pl.multiple_of(h * part, part), part)
        target_at = pl.ds(pl.multiple_of(half + h * part, part), part)
        for group in range(2):
            at = slice(group * rows, (group + 1) * rows)
            cols = slice(group * part, (group + 1) * part)
            out_ref[at, sum_at] = summed[:, cols]
            out_ref[at, target_at] = target[:, cols]
    swapped = core == 0
    extra = pack_extra(
        [
            unpack_extra(jnp.where(swapped, extras[1 - h], extras[h]), 1)[0]
            for h in range(2)
        ]
    ).astype(bf16)
    for group in range(2):
        out_ref[group * rows : (group + 1) * rows, width:] = extra


def pair_sum(where, *arrays):
    rows, half = arrays[1].shape
    return pl.pallas_call(
        pair_kernel,
        in_specs=[pl.BlockSpec(memory_space=pltpu.SMEM)]
        + [pl.BlockSpec(memory_space=pltpu.VMEM)] * len(arrays),
        out_shape=pltpu.VMEM((2 * rows, 2 * half + lanes), bf16),
        compiler_params=params(12),
        name="pair_sum",
    )(where, *arrays)


def home_kernel(where_ref, got_ref, unit_ref, len_ref, loss_ref, grad_ref):
    column = where_ref[2]
    images, part = grad_ref.shape
    half = images // 2
    summed = jnp.zeros((images, got_ref.shape[1]), f32)
    for k in range(0, got_ref.shape[0], images):
        summed = summed + got_ref[k : k + images, :].astype(f32)
    summed = summed[:half] + summed[half:]
    row = lax.broadcasted_iota(jnp.int32, (half, images), 0)
    lane = lax.broadcasted_iota(jnp.int32, (half, images), 1)
    loss_row = jnp.zeros((1, images), f32)
    for h, (rest, inner, cos) in enumerate(unpack_extra(summed[:, 4 * part :], 2)):
        at = slice(h * half, (h + 1) * half)
        gradient = summed[:, h * part : (h + 1) * part]
        target = summed[:, (2 + h) * part : (3 + h) * part]
        shifted, slope = arc_target(cos)
        own = jnp.exp(logit_scale * shifted)
        total = rest + own
        loss = jnp.log(total) - logit_scale * shifted
        loss_row += jnp.sum(jnp.where(lane == row + h * half, loss, 0.0), axis=0, keepdims=True)
        weight = (logit_scale * ((own / total - 1.0) * slope)).astype(bf16).astype(f32)
        scale = logit_scale / total
        dots = inner * scale + weight * cos
        unit = unit_ref[at, pl.ds(pl.multiple_of(column * part, part), part)]
        grad_ref[at, :] = (gradient * scale + weight * target - unit * dots) / len_ref[at, :1]
    loss_ref[...] = loss_row


def home(where, got, unit, length):
    images = unit.shape[0]
    part = unit.shape[1] // 4
    return pl.pallas_call(
        home_kernel,
        in_specs=[
            pl.BlockSpec(memory_space=pltpu.SMEM),
            pl.BlockSpec(memory_space=pltpu.VMEM),
            pl.BlockSpec(memory_space=pltpu.VMEM),
            pl.BlockSpec(memory_space=pltpu.VMEM),
        ],
        out_shape=(
            jax.ShapeDtypeStruct((1, images), f32),
            jax.ShapeDtypeStruct((images, part), f32),
        ),
        compiler_params=params(12),
        name="home",
    )(where, got, unit, length)


swap = [(0, 1), (1, 0)]


def shards(tokens, norm_gain, weight_in, weight_out, final_gain, centres, labels):
    images, tok_count, width = tokens.shape
    count = centres.shape[0]
    homes = lax.axis_size("dp")
    core = lax.axis_index("core")
    column = lax.axis_index("z_hi") * 2 + core
    offset = (column * homes + lax.axis_index("dp")) * count
    where = jnp.stack([offset, core, column]).astype(jnp.int32)

    partial = feed_forward(
        tokens.reshape(-1, width), norm_gain[None], weight_in, weight_out
    )
    partial = partial + lax.ppermute(partial, "core", swap)
    other = lax.ppermute(partial, "z_hi", swap)
    send, unit, length = unit_rows_of(where, labels, partial, other, final_gain[None], homes)
    gathered = lax.all_to_all(send, "dp", 0, 0, tiled=True)
    crossed = lax.ppermute(gathered, "core", swap)
    keep, keep_rows, give, inverse = class_pass(where, gathered, centres)
    got = lax.ppermute(give, "core", swap)
    keep_2, keep_rows_2, give_2 = class_pass(where, crossed, centres, inverse)
    got_2 = lax.ppermute(give_2, "core", swap)
    paired = pair_sum(where, keep, keep_rows, got_2, keep_2, keep_rows_2, got)
    arrived = lax.all_to_all(paired, ("z_hi", "dp"), 0, 0, tiled=True)
    loss, grad = home(where, arrived, unit, length)
    return (loss[0], grad)


def solution(mesh):
    fine = Mesh(mesh.devices.reshape(2, 2, -1), ("z_hi", "core", "dp"))
    mp = ("z_hi", "core")
    return jax.shard_map(
        shards,
        mesh=fine,
        in_specs=(
            P("dp", None, None),
            P(),
            P(None, mp),
            P(mp, None),
            P(),
            P((*mp, "dp"), None),
            P("dp"),
        ),
        out_specs=(P("dp"), P("dp", mp)),
        check_vma=False,
    )
```

```python
import functools
import math

import jax
import jax.numpy as jnp
from jax import lax
from jax.experimental import pallas as pl
from jax.experimental.pallas import tpu as pltpu
from jax.sharding import Mesh, PartitionSpec as P

logit_scale = 64.0
angle_margin = 0.5
exp2_scale = logit_scale / math.log(2.0)
lanes = 128
digits = 3
pieces = 8
columns = 256
batch = 4
f32 = jnp.float32
bf16 = jnp.bfloat16


def params(mebibytes):
    return pltpu.CompilerParams(vmem_limit_bytes=mebibytes * 1024 * 1024)


def arc_target(target_cos):
    target_sine = jnp.sqrt(jnp.maximum(1.0 - target_cos * target_cos, 0.01))
    inside = target_cos > -math.cos(angle_margin)
    shifted = jnp.where(
        inside,
        target_cos * math.cos(angle_margin) - target_sine * math.sin(angle_margin),
        target_cos - angle_margin * math.sin(angle_margin),
    )
    margin_slope = jnp.where(
        inside, math.cos(angle_margin) + math.sin(angle_margin) * target_cos / target_sine, 1.0
    )
    return (shifted, margin_slope)


def layer_norm(values, gain_vec):
    average = jnp.mean(values, axis=-1, keepdims=True)
    centred = values - average
    variance = jnp.mean(centred * centred, axis=-1, keepdims=True)
    return centred * lax.rsqrt(variance + 1e-06) * gain_vec


def split3(value):
    hi = value.astype(bf16).astype(f32)
    mid = (value - hi).astype(bf16).astype(f32)
    return hi, mid, value - hi - mid


toks = 64


def ffn_kernel(tokens_ref, gain_ref, win_ref, wout_hbm, out_ref, mean_ref, tok_ref, wout, sem):
    step = pl.program_id(0)
    block, width = tokens_ref.shape
    sub = 256
    per = sub // toks
    fetch = pltpu.make_async_copy(wout_hbm, wout, sem)

    @pl.when(step == 0)
    def _():
        fetch.start()

    image = lax.broadcasted_iota(jnp.int32, (8, sub), 0)
    member = (lax.broadcasted_iota(jnp.int32, (8, sub), 1) // toks == image).astype(f32).astype(bf16)
    for k in range(block // sub):
        rows = tokens_ref[k * sub : (k + 1) * sub, :]
        normed = layer_norm(rows.astype(f32), gain_ref[...]).astype(bf16)
        pre = jnp.dot(normed, win_ref[...], preferred_element_type=f32)
        hidden = (0.5 * pre * (1.0 + lax.erf(pre * math.sqrt(0.5)))).astype(bf16)
        mean = jnp.dot(member, hidden, preferred_element_type=f32) * (1.0 / toks)
        tok = jnp.dot(member, rows, preferred_element_type=f32) * (0.25 / toks)
        for q in range(per):
            at = pl.ds(step * (block // toks) + k * per + q, 1)
            mean_ref[at, :] = mean[q : q + 1]
            tok_ref[at, :] = tok[q : q + 1]

    @pl.when(step == pl.num_programs(0) - 1)
    def _():
        fetch.wait()
        mean = mean_ref[...]
        hi = mean.astype(bf16)
        lo = (mean - hi.astype(f32)).astype(bf16)
        both = jnp.dot(jnp.concatenate([hi, lo], axis=0), wout[...], preferred_element_type=f32)
        images = mean.shape[0]
        out_ref[...] = both[:images] + both[images:] + tok_ref[...]


def feed_forward(tokens, gain, weight_in, weight_out):
    rows, width = tokens.shape
    hidden = weight_in.shape[1]
    images = rows // toks
    block = 512
    return pl.pallas_call(
        ffn_kernel,
        grid=(rows // block,),
        in_specs=[
            pl.BlockSpec((block, width), lambda i: (i, 0)),
            pl.BlockSpec((1, width), lambda i: (0, 0)),
            pl.BlockSpec((width, hidden), lambda i: (0, 0)),
            pl.BlockSpec(memory_space=pltpu.HBM),
        ],
        out_specs=pl.BlockSpec((images, width), lambda i: (0, 0)),
        out_shape=pltpu.VMEM((images, width), f32),
        scratch_shapes=[
            pltpu.VMEM((images, hidden), f32),
            pltpu.VMEM((images, width), f32),
            pltpu.VMEM((hidden, width), bf16),
            pltpu.SemaphoreType.DMA,
        ],
        compiler_params=params(58),
        cost_estimate=pl.CostEstimate(
            flops=2 * rows * width * hidden, bytes_accessed=6 << 20, transcendentals=rows * hidden
        ),
        name="ffn",
    )(tokens, gain, weight_in, weight_out)


def unit_kernel(where_ref, labels_ref, mine_ref, other_ref, gain_ref, send_ref, unit_ref, len_ref):
    images, width = mine_ref.shape
    pooled = mine_ref[...] + other_ref[...]
    embedding = layer_norm(pooled, gain_ref[...])
    length = jnp.sqrt(jnp.sum(embedding * embedding, axis=1, keepdims=True) + 1e-06)
    unit = (embedding / length).astype(bf16).astype(f32)
    half = images // 2
    first = where_ref[1] == 1
    row = lax.broadcasted_iota(jnp.int32, (half, lanes), 0)
    lane = lax.broadcasted_iota(jnp.int32, (half, lanes), 1)
    label = jnp.zeros((half, lanes), jnp.int32)
    for r in range(half):
        label = jnp.where(
            row == r, jnp.where(first, labels_ref[r], labels_ref[half + r]), label
        )
    coded = jnp.where(
        lane == 0,
        label & 127,
        jnp.where(lane == 1, (label >> 7) & 127, jnp.where(lane == 2, label >> 14, 0)),
    )
    chosen = jnp.where(first, unit[:half], unit[half:])
    payload = jnp.concatenate([chosen, coded.astype(f32)], axis=1)
    payload = jnp.concatenate([payload, payload], axis=0).astype(bf16)
    for d in range(send_ref.shape[0] // images):
        send_ref[d * images : (d + 1) * images, :] = payload
    unit_ref[...] = unit
    len_ref[...] = jnp.broadcast_to(length, (images, lanes))


def unit_rows_of(where, labels, mine, other, gain, homes):
    images, width = mine.shape
    return pl.pallas_call(
        unit_kernel,
        in_specs=[
            pl.BlockSpec(memory_space=pltpu.SMEM),
            pl.BlockSpec(memory_space=pltpu.SMEM),
            pl.BlockSpec(memory_space=pltpu.VMEM),
            pl.BlockSpec(memory_space=pltpu.VMEM),
            pl.BlockSpec(memory_space=pltpu.VMEM),
        ],
        out_shape=(
            pltpu.VMEM((homes * images // 2, width + lanes), bf16),
            jax.ShapeDtypeStruct((images, width), f32),
            jax.ShapeDtypeStruct((images, lanes), f32),
        ),
        compiler_params=params(8),
        name="unit_rows",
    )(where, labels, mine, other, gain)


def digit_weights(shape, axis):
    at = lax.broadcasted_iota(jnp.int32, shape, axis)
    return jnp.where(
        at == 0, 1.0, jnp.where(at == 1, 128.0, jnp.where(at == 2, 16384.0, 0.0))
    ).astype(bf16)


group_size = 16


def class_kernel(second, where_ref, all_ref, centres_ref, *refs):
    if second:
        inverse_ref, keep_ref, keep_row_ref, send_ref, *refs = refs
    else:
        keep_ref, keep_row_ref, send_ref, inverse_ref, *refs = refs
    held, acc, tot, cos_row, lab, lab_s, found_s, lab_sem, sems = refs
    offset, core = where_ref[0], where_ref[1]
    images = all_ref.shape[0]
    count, width = centres_ref.shape
    piece = count // pieces
    half, part = width // 2, width // 4
    groups = images // group_size

    def fetch(i):
        at = pl.ds(pl.multiple_of(i * piece, piece), piece)
        return pltpu.make_async_copy(centres_ref.at[at, :], held.at[at, :], sems.at[i])

    for i in range(3):
        fetch(i).start()

    coded = all_ref[:, width:]
    turned = (((1,), (1,)), ((), ()))
    row = lax.dot_general(
        digit_weights((8, lanes), 1), coded, turned, preferred_element_type=f32
    ).astype(jnp.int32) - offset
    member = lax.broadcasted_iota(jnp.int32, (images, lanes), 0) // group_size
    member = (member == lax.broadcasted_iota(jnp.int32, (images, lanes), 1)).astype(bf16)
    inside = jnp.logical_and(row >= 0, row < count).astype(f32).astype(bf16)
    lab[:, :images] = row
    lab[:, images:] = jnp.dot(inside, member, preferred_element_type=f32).astype(jnp.int32)
    copy = pltpu.make_async_copy(lab, lab_s, lab_sem)
    copy.start()
    local = (
        jnp.dot(coded, digit_weights((lanes, lanes), 0), preferred_element_type=f32)
    ).astype(jnp.int32) - offset
    acc[...] = jnp.zeros(acc.shape, f32)
    tot[...] = jnp.zeros(tot.shape, f32)
    cos_row[...] = jnp.zeros(cos_row.shape, f32)
    keep_row_ref[...] = jnp.zeros(keep_row_ref.shape, bf16)
    send_ref[:, half:width] = jnp.zeros((images, half), bf16)
    copy.wait()
    found_s[images] = 0

    def look(g, c):
        @pl.when(lab_s[0, images + g] > 0)
        def _():
            for k in range(group_size):
                i = g * group_size + k
                at = lab_s[0, i]

                @pl.when(jnp.logical_and(at >= 0, at < count))
                def _():
                    n = found_s[images]
                    found_s[n] = i
                    found_s[images] = n + 1

        return c

    lax.fori_loop(0, groups, look, 0)

    diagonal = lax.broadcasted_iota(jnp.int32, (lanes, lanes), 0) == lax.broadcasted_iota(
        jnp.int32, (lanes, lanes), 1
    )

    def step(first, joined, ahead):
        base = pl.multiple_of(first * piece, piece)
        block = joined * piece
        for q in range(joined):
            fetch(first + q).wait()
        for q in ahead:
            fetch(first + q).start()

        centres = held[pl.ds(base, block), :]
        cosine = lax.dot_general(
            all_ref[:, :width], centres, turned, preferred_element_type=f32
        )
        lane = lax.broadcasted_iota(jnp.int32, (images, lanes), 1) + base
        parts = []
        total = tot[...]
        for j in range(block // lanes):
            at = pl.ds(base + j * lanes, lanes)
            if second:
                inverse = inverse_ref[:, at]
            else:
                wide = held[at, :].astype(f32)
                square = jnp.sum(wide * wide, axis=1, keepdims=True)
                square = jnp.sum(jnp.where(diagonal, square, 0.0), axis=0, keepdims=True)
                inverse = lax.rsqrt(square + 1e-06)
                inverse_ref[:, at] = inverse
            value = jnp.exp2(cosine[:, j * lanes : (j + 1) * lanes] * (inverse * exp2_scale))
            value = jnp.where(local == lane + j * lanes, 0.0, value)
            total = total + value
            parts.append((value * inverse).astype(bf16))
        tot[...] = total
        weight = jnp.concatenate(parts, axis=1)
        for n in range(0, width, columns):
            cols = slice(n, n + columns)
            acc[:, cols] += jnp.dot(weight, centres[:, cols], preferred_element_type=f32)

    def pair(t, c):
        step(1 + 2 * t, 2, (4, 5))
        return c

    step(0, 1, (3, 4))
    lax.fori_loop(0, (pieces - 6) // 2, pair, 0)
    step(pieces - 5, 2, (4,))
    step(pieces - 3, 2, ())
    step(pieces - 1, 1, ())

    sub = lax.broadcasted_iota(jnp.int32, (16, width), 0)

    def take(k, c):
        ready = []
        for q in range(batch):
            i = found_s[jnp.minimum(k * batch + q, found_s[images] - 1)]
            at = lab_s[0, i]
            raw = held[pl.ds(pl.multiple_of((at >> 4) << 4, 16), 16), :].astype(f32)
            raw = jnp.sum(jnp.where(sub == (at & 15), raw, 0.0), axis=0, keepdims=True)
            found = raw * lax.rsqrt(jnp.sum(raw * raw, axis=1, keepdims=True) + 1e-06)
            found = found.astype(bf16).astype(f32)
            mine = sub == (i & 15)
            here = pl.ds(pl.multiple_of((i >> 4) << 4, 16), 16)
            image = all_ref[here, :width].astype(f32)
            cos = jnp.sum(jnp.where(mine, image * found, 0.0), axis=1, keepdims=True)
            even = jnp.concatenate([found[:, :part], found[:, half : half + part]], axis=1)
            odd = jnp.concatenate([found[:, part:half], found[:, half + part :]], axis=1)
            kept = jnp.where(core == 0, even, odd)
            sent = jnp.where(core == 0, odd, even)
            ready.append((mine, here, cos, kept, sent))
        for mine, here, cos, kept, sent in ready:
            cos_row[here, :] = jnp.where(mine[:, :lanes], cos, cos_row[here, :])
            for ref, start, value in ((keep_row_ref, 0, kept), (send_ref, half, sent)):
                cols = slice(start, start + half)
                ref[here, cols] = jnp.where(
                    mine[:, :half], value, ref[here, cols].astype(f32)
                ).astype(bf16)
        return c

    lax.fori_loop(0, (found_s[images] + batch - 1) // batch, take, 0)

    for group in range(2):
        cols = slice(group * part, (group + 1) * part)
        keep_at = pl.multiple_of((2 * group + core) * part, part)
        send_at = pl.multiple_of((2 * group + 1 - core) * part, part)
        keep_ref[:, cols] = acc[:, pl.ds(keep_at, part)]
        send_ref[:, cols] = acc[:, pl.ds(send_at, part)].astype(bf16)
    total = jnp.sum(tot[...], axis=1, keepdims=True)
    inner = jnp.sum(acc[...] * all_ref[:, :width].astype(f32), axis=1, keepdims=True)
    extra = pack_extra([(total, inner, cos_row[:, :1])])
    keep_ref[:, half:] = extra
    send_ref[:, width:] = extra.astype(bf16)


def pack_extra(halves):
    shape = (halves[0][0].shape[0], lanes)
    lane = lax.broadcasted_iota(jnp.int32, shape, 1)
    out = jnp.zeros(shape, f32)
    k = 0
    for values in halves:
        for value in values:
            for piece in split3(value):
                out = jnp.where(lane == k, piece, out)
                k += 1
    return out


def unpack_extra(extra):
    lane = lax.broadcasted_iota(jnp.int32, extra.shape, 1)
    return [
        [
            jnp.sum(
                jnp.where(jnp.logical_and(lane // 64 == h, lane % 16 // 3 == k), extra, 0.0),
                axis=1,
                keepdims=True,
            )
            for k in range(3)
        ]
        for h in range(2)
    ]


def class_pass(where, gathered, centres, inverse=None):
    images = gathered.shape[0]
    count, width = centres.shape
    half = width // 2
    second = inverse is not None
    vmem = pl.BlockSpec(memory_space=pltpu.VMEM)
    outs = (
        jax.ShapeDtypeStruct((images, half + lanes), f32),
        jax.ShapeDtypeStruct((images, half), bf16),
        jax.ShapeDtypeStruct((images, width + lanes), bf16),
    )
    return pl.pallas_call(
        functools.partial(class_kernel, second),
        in_specs=[
            pl.BlockSpec(memory_space=pltpu.SMEM),
            vmem,
            pl.BlockSpec(memory_space=pltpu.HBM),
        ]
        + [vmem] * second,
        out_shape=outs if second else (*outs, jax.ShapeDtypeStruct((1, count), f32)),
        scratch_shapes=[
            pltpu.VMEM((count, width), bf16),
            pltpu.VMEM((images, width), f32),
            pltpu.VMEM((images, lanes), f32),
            pltpu.VMEM((images, lanes), f32),
            pltpu.VMEM((8, images + lanes), jnp.int32),
            pltpu.SMEM((8, images + lanes), jnp.int32),
            pltpu.SMEM((images + 1,), jnp.int32),
            pltpu.SemaphoreType.DMA,
            pltpu.SemaphoreType.DMA((pieces,)),
        ],
        compiler_params=params(48),
        cost_estimate=pl.CostEstimate(
            flops=4 * images * count * width,
            bytes_accessed=2 * count * width,
            transcendentals=images * count,
        ),
        name="class_pass",
    )(where, gathered, centres, *([inverse] if second else []))


def pair_kernel(where_ref, *refs):
    out_ref = refs[-1]
    rows, half = refs[1].shape
    width, part = 2 * half, half // 2
    sums, targets, extras = [], [], []
    for keep_ref, keep_row_ref, got_ref in (refs[0:3], refs[3:6]):
        sums.append((keep_ref[:, :half] + got_ref[:, :half].astype(f32)).astype(bf16))
        targets.append(keep_row_ref[...] + got_ref[:, half:width])
        extras.append(keep_ref[:, half:] + got_ref[:, width:].astype(f32))
    swapped = where_ref[1] == 0
    spread = []
    for h in range(2):
        hi, mid, low = split3(jnp.where(swapped, extras[1 - h], extras[h]))
        spread.append(hi + pltpu.roll(mid, 16, 1) + pltpu.roll(low, 32, 1))
    extra = (spread[0] + pltpu.roll(spread[1], 64, 1)).astype(bf16)
    for h in range(2):
        summed = jnp.where(swapped, sums[1 - h], sums[h])
        target = jnp.where(swapped, targets[1 - h], targets[h])
        for group in range(2):
            at = slice(group * rows, (group + 1) * rows)
            cols = slice(group * part, (group + 1) * part)
            out_ref[at, h * part : (h + 1) * part] = summed[:, cols]
            out_ref[at, half + h * part : half + (h + 1) * part] = target[:, cols]
    for group in range(2):
        out_ref[group * rows : (group + 1) * rows, width:] = extra


def pair_sum(where, *arrays):
    rows, half = arrays[1].shape
    return pl.pallas_call(
        pair_kernel,
        in_specs=[pl.BlockSpec(memory_space=pltpu.SMEM)]
        + [pl.BlockSpec(memory_space=pltpu.VMEM)] * len(arrays),
        out_shape=pltpu.VMEM((2 * rows, 2 * half + lanes), bf16),
        compiler_params=params(12),
        name="pair_sum",
    )(where, *arrays)


def home_kernel(where_ref, got_ref, unit_ref, len_ref, loss_ref, grad_ref):
    column = where_ref[2]
    images, part = grad_ref.shape
    half = images // 2
    summed = jnp.zeros((images, got_ref.shape[1]), f32)
    for k in range(0, got_ref.shape[0], images):
        summed = summed + got_ref[k : k + images, :].astype(f32)
    summed = summed[:half] + summed[half:]
    row = lax.broadcasted_iota(jnp.int32, (half, images), 0)
    lane = lax.broadcasted_iota(jnp.int32, (half, images), 1)
    loss_row = jnp.zeros((1, images), f32)
    for h, (rest, inner, cos) in enumerate(unpack_extra(summed[:, 4 * part :])):
        at = slice(h * half, (h + 1) * half)
        gradient = summed[:, h * part : (h + 1) * part]
        target = summed[:, (2 + h) * part : (3 + h) * part]
        shifted, slope = arc_target(cos)
        own = jnp.exp(logit_scale * shifted)
        total = rest + own
        loss = jnp.log(total) - logit_scale * shifted
        loss_row += jnp.sum(jnp.where(lane == row + h * half, loss, 0.0), axis=0, keepdims=True)
        weight = (logit_scale * ((own / total - 1.0) * slope)).astype(bf16).astype(f32)
        scale = logit_scale / total
        dots = inner * scale + weight * cos
        unit = unit_ref[at, pl.ds(pl.multiple_of(column * part, part), part)]
        grad_ref[at, :] = (gradient * scale + weight * target - unit * dots) / len_ref[at, :1]
    loss_ref[...] = loss_row


def home(where, got, unit, length):
    images = unit.shape[0]
    part = unit.shape[1] // 4
    return pl.pallas_call(
        home_kernel,
        in_specs=[
            pl.BlockSpec(memory_space=pltpu.SMEM),
            pl.BlockSpec(memory_space=pltpu.VMEM),
            pl.BlockSpec(memory_space=pltpu.VMEM),
            pl.BlockSpec(memory_space=pltpu.VMEM),
        ],
        out_shape=(
            jax.ShapeDtypeStruct((1, images), f32),
            jax.ShapeDtypeStruct((images, part), f32),
        ),
        compiler_params=params(12),
        name="home",
    )(where, got, unit, length)


swap = [(0, 1), (1, 0)]


def shards(tokens, norm_gain, weight_in, weight_out, final_gain, centres, labels):
    images, tok_count, width = tokens.shape
    count = centres.shape[0]
    homes = lax.axis_size("dp")
    core = lax.axis_index("core")
    column = lax.axis_index("z_hi") * 2 + core
    offset = (column * homes + lax.axis_index("dp")) * count
    where = jnp.stack([offset, core, column]).astype(jnp.int32)

    partial = feed_forward(
        tokens.reshape(-1, width), norm_gain[None], weight_in, weight_out
    )
    partial = partial + lax.ppermute(partial, "core", swap)
    other = lax.ppermute(partial, "z_hi", swap)
    send, unit, length = unit_rows_of(where, labels, partial, other, final_gain[None], homes)
    gathered = lax.all_to_all(send, "dp", 0, 0, tiled=True)
    crossed = lax.ppermute(gathered, "core", swap)
    keep, keep_rows, give, inverse = class_pass(where, gathered, centres)
    got = lax.ppermute(give, "core", swap)
    keep_2, keep_rows_2, give_2 = class_pass(where, crossed, centres, inverse)
    got_2 = lax.ppermute(give_2, "core", swap)
    paired = pair_sum(where, keep, keep_rows, got_2, keep_2, keep_rows_2, got)
    arrived = lax.all_to_all(paired, ("z_hi", "dp"), 0, 0, tiled=True)
    loss, grad = home(where, arrived, unit, length)
    return (loss[0], grad)


def solution(mesh):
    fine = Mesh(mesh.devices.reshape(2, 2, -1), ("z_hi", "core", "dp"))
    mp = ("z_hi", "core")
    return jax.shard_map(
        shards,
        mesh=fine,
        in_specs=(
            P("dp", None, None),
            P(),
            P(None, mp),
            P(mp, None),
            P(),
            P((*mp, "dp"), None),
            P("dp"),
        ),
        out_specs=(P("dp"), P("dp", mp)),
        check_vma=False,
    )
```
